32 devices in a mesh: slab: 8 (over z, x), tile: 4 (over y, core).
Axes of the slice: x: 2, y: 2, z: 4, core: 2. Of those that a mesh axis runs over, the one named last changes fastest.
Arguments:
- old_fine: float32 [2048, 5, 512], P(('slab', 'tile')), may hold values from -6 to 6
- coarse_fine: float32 [2048, 5, 64], P(('slab', 'tile')), may hold values from -6 to 6
- old_owner: int32 [8, 4, 64], P('slab', 'tile'), may hold values from 0 to 3, as said below
- new_refine: int32 [8, 4, 64], P('slab', 'tile'), may hold values from 0 to 1
- parent_map: int32 [8, 4, 64], P('slab', 'tile'), may hold values from 0 to 63
- courant: float32 [3, 5], replicated, may hold values from 0.05 to 0.3
Outputs:
- fine_next: float32 [5, 64, 128, 128], P(None, 'slab', 'tile')
The draws below stay inside these ranges and needn't reach their ends.
Inputs may be any that keep to these rules, and one draw needn't show every extreme that they name: `old_owner`: in each slab, old block k of tile t goes to tile (t + o_k) mod 4 with offsets o_k of the slab; every device sends exactly 16 blocks to each tile, and new slot k receives old slot k.
All inputs are finite; a program needn't handle non-finite values.
Results may differ from the reference program's by a relative error of at most 0.0003.
Values sent between devices are 32-bit elements; how exact they have to be, the bound alone decides.
A program may use at most 64 MiB of HBM per device.

```python
import math
import jax
import jax.numpy as jnp
from jax import lax

F = 5
E = 8
BX = 16
BY = 4
K_DEV = 64
BLOCKS = 2048
N_SLAB = 8
N_TILE = 4


def draw_old_owner(key, part):
    per_peer = K_DEV // N_TILE
    keys = jax.random.split(key, N_SLAB)

    def one_slab(slab_key):
        first, second = jax.random.split(slab_key)
        order = jax.random.permutation(first, K_DEV)
        start = jax.random.randint(second, (), 0, N_TILE)
        return (order // per_peer + start) % N_TILE
    offsets = jax.vmap(one_slab)(keys)
    tiles = jnp.arange(N_TILE)[None, :, None]
    return ((tiles + offsets[:, None, :]) % N_TILE).astype(jnp.int32)


def draw_new_refine(key, part):
    first, second = jax.random.split(jax.random.fold_in(key, 7))
    limit = jax.random.randint(first, (N_SLAB, N_TILE, 1), 10, 70)
    rolls = jax.random.randint(second, (N_SLAB, N_TILE, K_DEV), 0, 100)
    return (rolls < limit).astype(jnp.int32)


def set_ends(values, stream_key, least, top_value):
    place = [jax.random.randint(jax.random.fold_in(stream_key, axis), (), 0, length) for axis, length in enumerate(values.shape)]
    widest = values.shape.index(max(values.shape))
    next_to = place[:widest] + [(place[widest] + 1) % values.shape[widest]] + place[widest + 1:]
    return values.at[tuple(place)].set(least).at[tuple(next_to)].set(top_value)


def block_scale(own_key, extent, cuts, low, high):
    loudness, own = 1.0, jax.random.fold_in(own_key, 6)
    for axis_at, blocks in cuts:
        heights = jnp.exp(jax.random.uniform(jax.random.fold_in(own, axis_at), (blocks,), jnp.float32, low / len(cuts), high / len(cuts)))
        loudness = loudness * jnp.repeat(heights, extent[axis_at] // blocks).reshape([-1 if axis == axis_at else 1 for axis in range(len(extent))])
    return loudness


def gaussian(key, extent, deviation, reach, pieces=(), kind=jnp.bfloat16):
    loudness = block_scale(key, extent, pieces, -0.22, 0.18) if pieces else 1.0
    values = jax.random.normal(key, extent, jnp.float32) * deviation * loudness
    return jnp.minimum(jnp.maximum(values, -reach), reach).astype(kind)


def setup_inputs(seed: int = 0) -> dict:
    arg_keys = jax.random.split(jax.random.key(seed), 7)
    old_fine = gaussian(arg_keys[0], (BLOCKS, F, E**3), 1.0, 6.0, ((0, 32),), jnp.float32)
    coarse_fine = gaussian(arg_keys[1], (BLOCKS, F, (E // 2)**3), 1.0, 6.0, ((0, 32),), jnp.float32)
    old_owner = draw_old_owner(jax.random.fold_in(arg_keys[6], 71), 0)
    new_refine = draw_new_refine(jax.random.fold_in(arg_keys[6], 71), 0)
    parent_map = set_ends(jax.random.randint(arg_keys[4], (N_SLAB, N_TILE, K_DEV), 0, K_DEV), jax.random.fold_in(arg_keys[4], 1), 0, K_DEV - 1).astype(jnp.int32)
    courant = jnp.clip(jnp.exp(jax.random.uniform(arg_keys[5], (3, F), jnp.float32, math.log(0.05), math.log(0.3))), 0.05, 0.3)
    return dict(old_fine=old_fine, coarse_fine=coarse_fine, old_owner=old_owner, new_refine=new_refine, parent_map=parent_map, courant=courant)


def minmod(left, right):
    return 0.5 * (jnp.sign(left) + jnp.sign(right)) * jnp.minimum(jnp.abs(left), jnp.abs(right))


def slopes(cells, axis):
    width = [(0, 0)] * cells.ndim
    width[axis] = (1, 1)
    padded = jnp.pad(cells, width, mode="edge")
    size = cells.shape[axis]
    below = lax.slice_in_dim(padded, 0, size, axis=axis)
    above = lax.slice_in_dim(padded, 2, size + 2, axis=axis)
    return minmod(cells - below, above - cells)


def refine_block(cells):
    nd = cells.ndim
    slope_z = slopes(cells, nd - 3)
    slope_y = slopes(cells, nd - 2)
    slope_x = slopes(cells, nd - 1)
    sigma = jnp.array([-0.25, 0.25], jnp.float32)
    def spread(v):
        return v[..., :, None, :, None, :, None]
    offset = (spread(slope_z) * sigma[:, None, None, None, None] + spread(slope_y) * sigma[:, None, None]) + spread(slope_x) * sigma
    fine = spread(cells) + offset
    half = cells.shape[-1]
    return fine.reshape(cells.shape[:-3] + (2 * half, 2 * half, 2 * half))


def advance(padded, courant):
    fields, zp, yp, xp = padded.shape
    zn, yn, xn = zp - 4, yp - 4, xp - 4
    def cut(dz, dy, dx):
        return padded[:, 2 + dz:2 + dz + zn, 2 + dy:2 + dy + yn, 2 + dx:2 + dx + xn]
    center = cut(0, 0, 0)
    total = jnp.zeros_like(center)
    for axis, unit in enumerate(((1, 0, 0), (0, 1, 0), (0, 0, 1))):
        lower1 = cut(-unit[0], -unit[1], -unit[2])
        lower2 = cut(-2 * unit[0], -2 * unit[1], -2 * unit[2])
        upper1 = cut(unit[0], unit[1], unit[2])
        face_hi = center + 0.5 * minmod(center - lower1, upper1 - center)
        face_lo = lower1 + 0.5 * minmod(lower1 - lower2, center - lower1)
        total = total + courant[axis][:, None, None, None] * (face_hi - face_lo)
    return center - total


def reference(old_fine, coarse_fine, old_owner, new_refine, parent_map, courant):
    slabs, tiles, blocks = old_owner.shape
    fields = old_fine.shape[1]
    half = E // 2
    old5 = old_fine.reshape(slabs, tiles, blocks, fields, E ** 3)
    offsets = old_owner[:, 0, :] % tiles
    source = (jnp.arange(tiles, dtype=jnp.int32)[None, :, None] - offsets[:, None, :]) % tiles
    slab_idx = jnp.arange(slabs, dtype=jnp.int32)[:, None, None]
    slot_idx = jnp.arange(blocks, dtype=jnp.int32)[None, None, :]
    moved = old5[slab_idx, source.astype(jnp.int32), slot_idx]
    coarse5 = coarse_fine.reshape(slabs, tiles, blocks, fields, half ** 3)
    rolled = jnp.roll(coarse5, 1, axis=0)
    parents = jnp.take_along_axis(rolled, parent_map.astype(jnp.int32)[:, :, :, None, None], axis=2)
    interp = refine_block(parents.reshape(slabs, tiles, blocks, fields, half, half, half)).reshape(slabs, tiles, blocks, fields, E ** 3)
    refilled = jnp.where((new_refine == 1)[:, :, :, None, None], interp, moved)
    region = refilled.reshape(slabs, tiles, BY, BX, fields, E, E, E)
    region = region.transpose(4, 0, 5, 1, 2, 6, 3, 7).reshape(fields, slabs * E, tiles * BY * E, BX * E)
    padded = jnp.pad(region, ((0, 0), (2, 2), (2, 2), (2, 2)))
    def one_slab(index):
        window = lax.dynamic_slice_in_dim(padded, (index * E).astype(jnp.int32), E + 4, axis=1)
        return advance(window, courant)
    stepped = lax.map(one_slab, jnp.arange(slabs, dtype=jnp.int32))
    return stepped.transpose(1, 0, 2, 3, 4).reshape(fields, slabs * E, tiles * BY * E, BX * E)
```

```python
import functools

import jax
import jax.numpy as jnp
from jax import lax
from jax.experimental import pallas as pl
from jax.experimental.pallas import tpu as pltpu
from jax.sharding import PartitionSpec as P

E = 8
BX = 16
BY = 4
LANES = 128
ORDER = (3, 0, 1, 2)
MESH = pl.DeviceIdType.MESH


def minmod(a, b):
    return jnp.maximum(jnp.minimum(a, jnp.maximum(b, 0.0)), jnp.minimum(b, 0.0))


def split(x):
    high = x.astype(jnp.bfloat16)
    low = (x - high.astype(jnp.float32)).astype(jnp.bfloat16)
    return high, low


def pick(onehot2, x):
    high, low = split(x)
    return jnp.dot(onehot2, jnp.concatenate([high, low], axis=0), preferred_element_type=jnp.float32)


def iota(shape, dim):
    return lax.broadcasted_iota(jnp.int32, shape, dim)


def column(row):
    size = row.shape[1]
    diag = iota((size, size), 0) == iota((size, size), 1)
    return jnp.sum(jnp.where(diag, jnp.broadcast_to(row, (size, size)), 0.0), axis=1, keepdims=True)


def twice(onehot):
    half = jnp.where(onehot, 1.0, 0.0).astype(jnp.bfloat16)
    return jnp.concatenate([half, half], axis=1)


def refine_matrix(h):
    rows, cols = 2 * 64, 512
    i, j = iota((rows, cols), 0), iota((rows, cols), 1)
    parent = ((j >> 7) << 4) + (((j >> 4) & 3) << 2) + ((j >> 1) & 3) + h * 64
    match = jnp.where(i == parent, 1.0, 0.0)
    out = [match]
    for bit in (6, 3, 0):
        sign = jnp.where(((j >> bit) & 1) == 1, 0.25, -0.25)
        out.append(match * sign)
    return jnp.concatenate([m.astype(jnp.bfloat16) for m in out], axis=0)


def parent_slopes(c):
    lane = iota(c.shape, 1)
    out = [c]
    for bit in (4, 2, 0):
        step = 1 << bit
        inside = ((lane >> bit) & 3) != 0
        below = jnp.where(inside, c - pltpu.roll(c, step, 1), 0.0)
        above = pltpu.roll(below, LANES - step, 1)
        out.append(minmod(below, above))
    return out


def swap_lanes(rows):
    lane = iota(rows[0].shape, 1)
    rows = list(rows)
    for b in range(4):
        step = 8 << b
        upper = ((lane >> (3 + b)) & 1) == 1
        for i in range(16):
            if i & (1 << b):
                continue
            j = i | (1 << b)
            x, y = rows[i], rows[j]
            rows[i] = jnp.where(upper, pltpu.roll(y, step, 1), x)
            rows[j] = jnp.where(upper, y, pltpu.roll(x, LANES - step, 1))
    return rows


def step_x(u, c):
    lane = iota(u.shape, 1)
    first, last = lane == 0, lane == LANES - 1
    d = u - jnp.where(first, 0.0, pltpu.roll(u, 1, 1))
    above = jnp.where(last, -u, pltpu.roll(d, LANES - 1, 1))
    g = u + 0.5 * minmod(d, above)
    return c * (g - jnp.where(first, 0.0, pltpu.roll(g, 1, 1)))


def step_y(u, low2, low1, high, c):
    n = u.shape[0]
    row = iota(u.shape, 0)
    first, last = row == 0, row == n - 1
    d = u - jnp.where(first, low1, pltpu.roll(u, 1, 0))
    above = jnp.where(last, high - u, pltpu.roll(d, n - 1, 0))
    g = u + 0.5 * minmod(d, above)
    under = low1 + 0.5 * minmod(low1 - low2, d[0:1])
    return c * (g - jnp.where(first, under, pltpu.roll(g, 1, 0)))


def kernel(
    slabs, tiles, old_hbm, coarse_hbm, owner_ref, refine_ref, parent_ref, courant,
    out, old, coarse, csend, crecv, send, recv, matrix, interp, tmp, region,
    zlow, zhigh, ysend_up, ysend_down, ylow, yhigh,
    load_sem, csem, asend, arecv, zsem, ysend_sem, yrecv_sem,
):
    slab, tile = lax.axis_index("slab"), lax.axis_index("tile")
    fields, blocks, cells = old.shape
    groups = cells // LANES
    rows = BY * E
    share = blocks // tiles
    up, down = lax.rem(slab + 1, slabs), lax.rem(slab + slabs - 1, slabs)
    has_down, has_up = slab > 0, slab < slabs - 1
    has_left, has_right = tile > 0, tile < tiles - 1

    barrier = pltpu.get_barrier_semaphore()
    for s in (up, down):
        pl.semaphore_signal(barrier, inc=1, device_id={"slab": s}, device_id_type=MESH)
    for o in range(1, tiles):
        pl.semaphore_signal(
            barrier, inc=1, device_id={"tile": lax.rem(tile + o, tiles)}, device_id_type=MESH
        )
    load_old = pltpu.make_async_copy(old_hbm, old, load_sem.at[0])
    load_coarse = pltpu.make_async_copy(coarse_hbm, coarse, load_sem.at[1])
    load_coarse.start()
    load_old.start()

    offset = owner_ref[0] - tile
    offset = jnp.where(offset < 0, offset + tiles, offset).astype(jnp.float32)
    square = (blocks, blocks)
    same = column(offset) == jnp.broadcast_to(offset, square)
    earlier = iota(square, 0) < iota(square, 1)
    rank = jnp.sum(jnp.where(same & earlier, 1.0, 0.0), axis=0, keepdims=True)
    place = offset * share + rank
    pack = twice(iota(square, 0).astype(jnp.float32) == jnp.broadcast_to(place, square))
    unpack_at = column(place) == iota(square, 1).astype(jnp.float32)
    refine = column(refine_ref[0].astype(jnp.float32)) > 0.5
    unpack = twice(unpack_at & ~refine)
    parents = twice((column(parent_ref[0].astype(jnp.float32)) == iota(square, 1).astype(jnp.float32)) & refine)

    load_coarse.wait()
    for f in range(fields):
        csend[f // 2, :, (f % 2) * 64:(f % 2) * 64 + 64] = coarse[f]
    if fields % 2:
        csend[fields // 2, :, 64:] = jnp.zeros((blocks, 64), jnp.float32)

    pl.semaphore_wait(barrier, tiles + 1)
    send_coarse = pltpu.make_async_remote_copy(
        csend, crecv, csem.at[0], csem.at[1], device_id={"slab": up}, device_id_type=MESH
    )
    send_coarse.start()

    def exchange(g, o):
        return pltpu.make_async_remote_copy(
            send.at[g, :, o], recv.at[g, :, o], asend.at[g, o], arecv.at[g, o],
            device_id={"tile": lax.rem(tile + o, tiles)}, device_id_type=MESH,
        )

    load_old.wait()
    for g in ORDER:
        for f in range(fields):
            packed = pick(pack, old[f, :, g * LANES:(g + 1) * LANES])
            send[g, f] = packed.reshape(tiles, share, LANES)
            recv[g, f, 0] = packed[:share]
        for o in sorted(range(1, tiles), key=lambda o: -min(o, tiles - o)):
            exchange(g, o).start()

    @pl.when(jnp.logical_not(has_down))
    def _():
        zlow[...] = jnp.zeros_like(zlow)

    @pl.when(jnp.logical_not(has_up))
    def _():
        zhigh[...] = jnp.zeros_like(zhigh)

    @pl.when(jnp.logical_not(has_left))
    def _():
        ylow[...] = jnp.zeros_like(ylow)

    @pl.when(jnp.logical_not(has_right))
    def _():
        yhigh[...] = jnp.zeros_like(yhigh)

    for h in range(2):
        matrix[h] = refine_matrix(h)
    send_coarse.wait_recv()
    for p in range(csend.shape[0]):
        parts = [split(part) for part in parent_slopes(pick(parents, crecv[p]))]
        high = jnp.concatenate([part[0] for part in parts], axis=1)
        low = jnp.concatenate([part[1] for part in parts], axis=1)
        for h in range(2):
            if 2 * p + h < fields:
                interp[2 * p + h] = jnp.dot(
                    high, matrix[h], preferred_element_type=jnp.float32
                ) + jnp.dot(low, matrix[h], preferred_element_type=jnp.float32)

    send_up = pltpu.make_async_remote_copy(
        region.at[E - 2:E], zlow, zsem.at[0], zsem.at[1], device_id={"slab": up}, device_id_type=MESH
    )
    send_down = pltpu.make_async_remote_copy(
        region.at[0:1], zhigh, zsem.at[2], zsem.at[3], device_id={"slab": down}, device_id_type=MESH
    )

    def send_right(g):
        return pltpu.make_async_remote_copy(
            ysend_up.at[2 * g:2 * g + 2], ylow.at[2 * g:2 * g + 2], ysend_sem.at[0, g], yrecv_sem.at[0, g],
            device_id={"tile": lax.rem(tile + 1, tiles)}, device_id_type=MESH,
        )

    def send_left(g):
        return pltpu.make_async_remote_copy(
            ysend_down.at[2 * g:2 * g + 2], yhigh.at[2 * g:2 * g + 2], ysend_sem.at[1, g], yrecv_sem.at[1, g],
            device_id={"tile": lax.rem(tile + tiles - 1, tiles)}, device_id_type=MESH,
        )

    def field_rows(f):
        return pl.ds(pl.multiple_of(f * rows, rows), rows)

    for g in ORDER:
        for o in range(1, tiles):
            exchange(g, o).wait_recv()
        for f in range(fields):
            moved = pick(unpack, recv[g, f].reshape(blocks, LANES))
            tmp[g, f * blocks:(f + 1) * blocks] = moved + interp[f, :, g * LANES:(g + 1) * LANES]
        turned = swap_lanes([tmp[g, pl.ds(b, fields * BY, stride=BX), :] for b in range(BX)])
        for j in range(BX):
            region[2 * g + j // E, pl.ds(j % E, fields * BY, stride=E), :] = turned[j]
        if g == 3:
            pl.when(has_up)(send_up.start)
        if g == 0:
            pl.when(has_down)(send_down.start)
        for z in (2 * g, 2 * g + 1):
            for i in range(2):
                ysend_up[z, i] = region[z, pl.ds(rows - 2 + i, fields, stride=rows), :]
            ysend_down[z, 0] = region[z, pl.ds(0, fields, stride=rows), :]
        pl.when(has_right)(send_right(g).start)
        pl.when(has_left)(send_left(g).start)

        def along_x(f, carry, g=g):
            for z in (2 * g, 2 * g + 1):
                u = region[z, field_rows(f), :]
                out[f, z] = u - step_x(u, courant[2, f])
            return carry

        lax.fori_loop(0, fields, along_x, 0)

    def along_z(f, carry):
        c = courant[0, f]
        u = [region[z, field_rows(f), :] for z in range(E)]
        d = [None] + [u[z] - u[z - 1] for z in range(1, E)]
        g = [None] + [u[z] + 0.5 * minmod(d[z], d[z + 1]) for z in range(1, E - 1)]
        for z in range(2, E - 1):
            out[f, z] -= c * (g[z] - g[z - 1])
        return carry

    lax.fori_loop(0, fields, along_z, 0)

    for g in ORDER:
        pl.when(has_left)(send_right(g).wait_recv)
        pl.when(has_right)(send_left(g).wait_recv)

    for z in range(E):
        for f in range(fields):
            u = region[z, f * rows:(f + 1) * rows, :]
            out[f, z] -= step_y(
                u, ylow[z, 0, f:f + 1], ylow[z, 1, f:f + 1], yhigh[z, 0, f:f + 1], courant[1, f]
            )

    pl.when(has_down)(send_up.wait_recv)
    pl.when(has_up)(send_down.wait_recv)

    def edges(f, carry):
        c = courant[0, f]
        at = field_rows(f)
        u = {z: region[z, at, :] for z in (0, 1, 2, E - 3, E - 2, E - 1)}
        u[-2], u[-1], u[E] = zlow[0, at, :], zlow[1, at, :], zhigh[0, at, :]
        d = {z: u[z] - u[z - 1] for z in (-1, 0, 1, 2, E - 2, E - 1, E)}
        g = {z: u[z] + 0.5 * minmod(d[z], d[z + 1]) for z in (-1, 0, 1, E - 2, E - 1)}
        for z in (0, 1, E - 1):
            out[f, z] -= c * (g[z] - g[z - 1])
        return carry

    lax.fori_loop(0, fields, edges, 0)

    send_coarse.wait_send()
    for g in ORDER:
        for o in range(1, tiles):
            exchange(g, o).wait_send()
        pl.when(has_right)(send_right(g).wait_send)
        pl.when(has_left)(send_left(g).wait_send)
    pl.when(has_up)(send_up.wait_send)
    pl.when(has_down)(send_down.wait_send)


def local(slabs, tiles, old_fine, coarse_fine, old_owner, new_refine, parent_map, courant):
    blocks, fields, cells = old_fine.shape
    half = coarse_fine.shape[2]
    groups = cells // LANES
    share = blocks // tiles
    rows = BY * E
    pairs = -(-fields // 2)
    f32 = jnp.float32
    vmem = pl.BlockSpec(memory_space=pltpu.VMEM)
    anywhere = pl.BlockSpec(memory_space=pl.ANY)
    dma = pltpu.SemaphoreType.DMA
    return pl.pallas_call(
        functools.partial(kernel, slabs, tiles),
        out_shape=jax.ShapeDtypeStruct((fields, E, rows, BX * E), f32),
        in_specs=[anywhere, anywhere, vmem, vmem, vmem, pl.BlockSpec(memory_space=pltpu.SMEM)],
        out_specs=vmem,
        scratch_shapes=[
            pltpu.VMEM((fields, blocks, cells), f32),
            pltpu.VMEM((fields, blocks, half), f32),
            pltpu.VMEM((pairs, blocks, LANES), f32),
            pltpu.VMEM((pairs, blocks, LANES), f32),
            pltpu.VMEM((groups, fields, tiles, share, LANES), f32),
            pltpu.VMEM((groups, fields, tiles, share, LANES), f32),
            pltpu.VMEM((2, 4 * LANES, cells), jnp.bfloat16),
            pltpu.VMEM((fields, blocks, cells), f32),
            pltpu.VMEM((groups, fields * blocks, LANES), f32),
            pltpu.VMEM((E, fields * rows, LANES), f32),
            pltpu.VMEM((2, fields * rows, LANES), f32),
            pltpu.VMEM((1, fields * rows, LANES), f32),
            pltpu.VMEM((E, 2, fields, LANES), f32),
            pltpu.VMEM((E, 1, fields, LANES), f32),
            pltpu.VMEM((E, 2, fields, LANES), f32),
            pltpu.VMEM((E, 1, fields, LANES), f32),
            dma((2,)),
            dma((2,)),
            dma((groups, tiles)),
            dma((groups, tiles)),
            dma((4,)),
            dma((2, groups)),
            dma((2, groups)),
        ],
        compiler_params=pltpu.CompilerParams(
            collective_id=0, has_side_effects=True, vmem_limit_bytes=40 * 1024 * 1024
        ),
        cost_estimate=pl.CostEstimate(flops=20_000_000, bytes_accessed=2_000_000, transcendentals=0),
    )(
        jnp.transpose(old_fine, (1, 0, 2)),
        jnp.transpose(coarse_fine, (1, 0, 2)),
        old_owner,
        new_refine,
        parent_map,
        courant,
    )


def solution(mesh):
    in_specs = (
        P(("slab", "tile"), None, None),
        P(("slab", "tile"), None, None),
        P("slab", "tile", None),
        P("slab", "tile", None),
        P("slab", "tile", None),
        P(),
    )
    out_specs = P(None, "slab", "tile", None)
    body = functools.partial(local, mesh.shape["slab"], mesh.shape["tile"])
    return jax.shard_map(body, mesh=mesh, in_specs=in_specs, out_specs=out_specs, check_vma=False)
```

```python
import functools

import jax
import jax.numpy as jnp
from jax import lax
from jax.experimental import pallas as pl
from jax.experimental.pallas import tpu as pltpu
from jax.sharding import PartitionSpec as P

E = 8
BX = 16
BY = 4
LANES = 128
ORDER = (3, 0, 1, 2)
MESH = pl.DeviceIdType.MESH


def minmod(a, b):
    return jnp.maximum(jnp.minimum(a, jnp.maximum(b, 0.0)), jnp.minimum(b, 0.0))


def split(x):
    high = x.astype(jnp.bfloat16)
    low = (x - high.astype(jnp.float32)).astype(jnp.bfloat16)
    return high, low


def pick(onehot2, x):
    high, low = split(x)
    return jnp.dot(onehot2, jnp.concatenate([high, low], axis=0), preferred_element_type=jnp.float32)


def iota(shape, dim):
    return lax.broadcasted_iota(jnp.int32, shape, dim)


def column(row):
    size = row.shape[1]
    diag = iota((size, size), 0) == iota((size, size), 1)
    return jnp.sum(jnp.where(diag, jnp.broadcast_to(row, (size, size)), 0.0), axis=1, keepdims=True)


def twice(onehot):
    half = jnp.where(onehot, 1.0, 0.0).astype(jnp.bfloat16)
    return jnp.concatenate([half, half], axis=1)


def refine_matrix(h):
    rows, cols = 2 * 64, 512
    i, j = iota((rows, cols), 0), iota((rows, cols), 1)
    parent = ((j >> 7) << 4) + (((j >> 4) & 3) << 2) + ((j >> 1) & 3) + h * 64
    match = jnp.where(i == parent, 1.0, 0.0)
    out = [match]
    for bit in (6, 3, 0):
        sign = jnp.where(((j >> bit) & 1) == 1, 0.25, -0.25)
        out.append(match * sign)
    return jnp.concatenate([m.astype(jnp.bfloat16) for m in out], axis=0)


def parent_slopes(c):
    lane = iota(c.shape, 1)
    out = [c]
    for bit in (4, 2, 0):
        step = 1 << bit
        inside = ((lane >> bit) & 3) != 0
        below = jnp.where(inside, c - pltpu.roll(c, step, 1), 0.0)
        above = pltpu.roll(below, LANES - step, 1)
        out.append(minmod(below, above))
    return out


def swap_lanes(rows):
    lane = iota(rows[0].shape, 1)
    rows = list(rows)
    for b in range(4):
        step = 8 << b
        upper = ((lane >> (3 + b)) & 1) == 1
        for i in range(16):
            if i & (1 << b):
                continue
            j = i | (1 << b)
            x, y = rows[i], rows[j]
            rows[i] = jnp.where(upper, pltpu.roll(y, step, 1), x)
            rows[j] = jnp.where(upper, y, pltpu.roll(x, LANES - step, 1))
    return rows


def step_x(u, c):
    lane = iota(u.shape, 1)
    first, last = lane == 0, lane == LANES - 1
    d = u - jnp.where(first, 0.0, pltpu.roll(u, 1, 1))
    above = jnp.where(last, -u, pltpu.roll(d, LANES - 1, 1))
    g = u + 0.5 * minmod(d, above)
    return c * (g - jnp.where(first, 0.0, pltpu.roll(g, 1, 1)))


def step_y(u, low2, low1, high, c):
    n = u.shape[0]
    row = iota(u.shape, 0)
    first, last = row == 0, row == n - 1
    d = u - jnp.where(first, low1, pltpu.roll(u, 1, 0))
    above = jnp.where(last, high - u, pltpu.roll(d, n - 1, 0))
    g = u + 0.5 * minmod(d, above)
    under = low1 + 0.5 * minmod(low1 - low2, d[0:1])
    return c * (g - jnp.where(first, under, pltpu.roll(g, 1, 0)))


def kernel(
    slabs, tiles, old_hbm, coarse_hbm, owner_hbm, refine_hbm, parent_hbm, courant_hbm,
    out, owner_ref, refine_ref, parent_ref, courant, old, coarse, csend, crecv, send, recv, matrix, interp, tmp, region,
    zlow, zhigh, ysend_up, ysend_down, ylow, yhigh,
    load_sem, csem, asend, arecv, zsem, ysend_sem, yrecv_sem,
):
    slab, tile = lax.axis_index("slab"), lax.axis_index("tile")
    fields, blocks, cells = old.shape
    groups = cells // LANES
    rows = BY * E
    share = blocks // tiles
    up, down = lax.rem(slab + 1, slabs), lax.rem(slab + slabs - 1, slabs)
    has_down, has_up = slab > 0, slab < slabs - 1
    has_left, has_right = tile > 0, tile < tiles - 1

    barrier = pltpu.get_barrier_semaphore()
    for s in (up, down):
        pl.semaphore_signal(barrier, inc=1, device_id={"slab": s}, device_id_type=MESH)
    for o in range(1, tiles):
        pl.semaphore_signal(
            barrier, inc=1, device_id={"tile": lax.rem(tile + o, tiles)}, device_id_type=MESH
        )
    sources = (owner_hbm, refine_hbm, parent_hbm, courant_hbm, coarse_hbm)
    targets = (owner_ref, refine_ref, parent_ref, courant, coarse)
    loads = [pltpu.make_async_copy(a, b, load_sem.at[i]) for i, (a, b) in enumerate(zip(sources, targets))]
    for load in loads:
        load.start()

    def load_old(g):
        at = pl.ds(g * LANES, LANES)
        return pltpu.make_async_copy(old_hbm.at[:, :, at], old.at[:, :, at], load_sem.at[5 + g])

    for g in ORDER:
        load_old(g).start()
    for load in loads[:3]:
        load.wait()

    offset = owner_ref[0] - tile
    offset = jnp.where(offset < 0, offset + tiles, offset).astype(jnp.float32)
    square = (blocks, blocks)
    same = column(offset) == jnp.broadcast_to(offset, square)
    earlier = iota(square, 0) < iota(square, 1)
    rank = jnp.sum(jnp.where(same & earlier, 1.0, 0.0), axis=0, keepdims=True)
    place = offset * share + rank
    pack = twice(iota(square, 0).astype(jnp.float32) == jnp.broadcast_to(place, square))
    unpack_at = column(place) == iota(square, 1).astype(jnp.float32)
    refine = column(refine_ref[0].astype(jnp.float32)) > 0.5
    unpack = twice(unpack_at & ~refine)
    parents = twice((column(parent_ref[0].astype(jnp.float32)) == iota(square, 1).astype(jnp.float32)) & refine)

    loads[4].wait()
    for f in range(fields):
        csend[f // 2, :, (f % 2) * 64:(f % 2) * 64 + 64] = coarse[f]
    if fields % 2:
        csend[fields // 2, :, 64:] = jnp.zeros((blocks, 64), jnp.float32)

    pl.semaphore_wait(barrier, tiles + 1)
    send_coarse = pltpu.make_async_remote_copy(
        csend, crecv, csem.at[0], csem.at[1], device_id={"slab": up}, device_id_type=MESH
    )
    send_coarse.start()

    def exchange(g, o):
        return pltpu.make_async_remote_copy(
            send.at[g, :, o], recv.at[g, :, o], asend.at[g, o], arecv.at[g, o],
            device_id={"tile": lax.rem(tile + o, tiles)}, device_id_type=MESH,
        )

    def send_group(g):
        for o in sorted(range(1, tiles), key=lambda o: -min(o, tiles - o)):
            exchange(g, o).start()

    def sent_group(g):
        for o in range(1, tiles):
            exchange(g, o).wait_send()

    loads[3].wait()
    for n, g in enumerate(ORDER):
        load_old(g).wait()
        for f in range(fields):
            packed = pick(pack, old[f, :, g * LANES:(g + 1) * LANES])
            send[g, f] = packed.reshape(tiles, share, LANES)
            recv[g, f, 0] = packed[:share]
        if n < 2:
            send_group(g)

    @pl.when(jnp.logical_not(has_down))
    def _():
        zlow[...] = jnp.zeros_like(zlow)

    @pl.when(jnp.logical_not(has_up))
    def _():
        zhigh[...] = jnp.zeros_like(zhigh)

    @pl.when(jnp.logical_not(has_left))
    def _():
        ylow[...] = jnp.zeros_like(ylow)

    @pl.when(jnp.logical_not(has_right))
    def _():
        yhigh[...] = jnp.zeros_like(yhigh)

    for h in range(2):
        matrix[h] = refine_matrix(h)
    sent_group(ORDER[0])
    send_group(ORDER[2])
    send_coarse.wait_recv()
    for p in range(csend.shape[0]):
        parts = [split(part) for part in parent_slopes(pick(parents, crecv[p]))]
        high = jnp.concatenate([part[0] for part in parts], axis=1)
        low = jnp.concatenate([part[1] for part in parts], axis=1)
        for h in range(2):
            if 2 * p + h < fields:
                interp[2 * p + h] = jnp.dot(
                    high, matrix[h], preferred_element_type=jnp.float32
                ) + jnp.dot(low, matrix[h], preferred_element_type=jnp.float32)

    sent_group(ORDER[1])
    send_group(ORDER[3])
    send_up = pltpu.make_async_remote_copy(
        region.at[E - 2:E], zlow, zsem.at[0], zsem.at[1], device_id={"slab": up}, device_id_type=MESH
    )
    send_down = pltpu.make_async_remote_copy(
        region.at[0:1], zhigh, zsem.at[2], zsem.at[3], device_id={"slab": down}, device_id_type=MESH
    )

    def send_right(g):
        return pltpu.make_async_remote_copy(
            ysend_up.at[2 * g:2 * g + 2], ylow.at[2 * g:2 * g + 2], ysend_sem.at[0, g], yrecv_sem.at[0, g],
            device_id={"tile": lax.rem(tile + 1, tiles)}, device_id_type=MESH,
        )

    def send_left(g):
        return pltpu.make_async_remote_copy(
            ysend_down.at[2 * g:2 * g + 2], yhigh.at[2 * g:2 * g + 2], ysend_sem.at[1, g], yrecv_sem.at[1, g],
            device_id={"tile": lax.rem(tile + tiles - 1, tiles)}, device_id_type=MESH,
        )

    def field_rows(f):
        return pl.ds(pl.multiple_of(f * rows, rows), rows)

    for g in ORDER:
        for o in range(1, tiles):
            exchange(g, o).wait_recv()
        for f in range(fields):
            moved = pick(unpack, recv[g, f].reshape(blocks, LANES))
            tmp[g, f * blocks:(f + 1) * blocks] = moved + interp[f, :, g * LANES:(g + 1) * LANES]
        turned = swap_lanes([tmp[g, pl.ds(b, fields * BY, stride=BX), :] for b in range(BX)])
        for j in range(BX):
            region[2 * g + j // E, pl.ds(j % E, fields * BY, stride=E), :] = turned[j]
        if g == 3:
            pl.when(has_up)(send_up.start)
        if g == 0:
            pl.when(has_down)(send_down.start)
        for z in (2 * g, 2 * g + 1):
            for i in range(2):
                ysend_up[z, i] = region[z, pl.ds(rows - 2 + i, fields, stride=rows), :]
            ysend_down[z, 0] = region[z, pl.ds(0, fields, stride=rows), :]
        pl.when(has_right)(send_right(g).start)
        pl.when(has_left)(send_left(g).start)

        def along_x(f, carry, g=g):
            for z in (2 * g, 2 * g + 1):
                u = region[z, field_rows(f), :]
                out[f, z] = u - step_x(u, courant[2, f])
            return carry

        lax.fori_loop(0, fields, along_x, 0)

    def along_z(f, carry):
        c = courant[0, f]
        u = [region[z, field_rows(f), :] for z in range(E)]
        d = [None] + [u[z] - u[z - 1] for z in range(1, E)]
        g = [None] + [u[z] + 0.5 * minmod(d[z], d[z + 1]) for z in range(1, E - 1)]
        for z in range(2, E - 1):
            out[f, z] -= c * (g[z] - g[z - 1])
        return carry

    lax.fori_loop(0, fields, along_z, 0)

    for g in ORDER:
        pl.when(has_left)(send_right(g).wait_recv)
        pl.when(has_right)(send_left(g).wait_recv)

    for z in range(E):
        for f in range(fields):
            u = region[z, f * rows:(f + 1) * rows, :]
            out[f, z] -= step_y(
                u, ylow[z, 0, f:f + 1], ylow[z, 1, f:f + 1], yhigh[z, 0, f:f + 1], courant[1, f]
            )

    pl.when(has_down)(send_up.wait_recv)
    pl.when(has_up)(send_down.wait_recv)

    def edges(f, carry):
        c = courant[0, f]
        at = field_rows(f)
        u = {z: region[z, at, :] for z in (0, 1, 2, E - 3, E - 2, E - 1)}
        u[-2], u[-1], u[E] = zlow[0, at, :], zlow[1, at, :], zhigh[0, at, :]
        d = {z: u[z] - u[z - 1] for z in (-1, 0, 1, 2, E - 2, E - 1, E)}
        g = {z: u[z] + 0.5 * minmod(d[z], d[z + 1]) for z in (-1, 0, 1, E - 2, E - 1)}
        for z in (0, 1, E - 1):
            out[f, z] -= c * (g[z] - g[z - 1])
        return carry

    lax.fori_loop(0, fields, edges, 0)

    send_coarse.wait_send()
    sent_group(ORDER[2])
    sent_group(ORDER[3])
    for g in ORDER:
        pl.when(has_right)(send_right(g).wait_send)
        pl.when(has_left)(send_left(g).wait_send)
    pl.when(has_up)(send_up.wait_send)
    pl.when(has_down)(send_down.wait_send)


def local(slabs, tiles, old_fine, coarse_fine, old_owner, new_refine, parent_map, courant):
    blocks, fields, cells = old_fine.shape
    half = coarse_fine.shape[2]
    groups = cells // LANES
    share = blocks // tiles
    rows = BY * E
    pairs = -(-fields // 2)
    f32 = jnp.float32
    vmem = pl.BlockSpec(memory_space=pltpu.VMEM)
    anywhere = pl.BlockSpec(memory_space=pl.ANY)
    dma = pltpu.SemaphoreType.DMA
    return pl.pallas_call(
        functools.partial(kernel, slabs, tiles),
        out_shape=jax.ShapeDtypeStruct((fields, E, rows, BX * E), f32),
        in_specs=[anywhere] * 6,
        out_specs=vmem,
        scratch_shapes=[
            pltpu.VMEM(old_owner.shape, jnp.int32),
            pltpu.VMEM(new_refine.shape, jnp.int32),
            pltpu.VMEM(parent_map.shape, jnp.int32),
            pltpu.SMEM(courant.shape, f32),
            pltpu.VMEM((fields, blocks, cells), f32),
            pltpu.VMEM((fields, blocks, half), f32),
            pltpu.VMEM((pairs, blocks, LANES), f32),
            pltpu.VMEM((pairs, blocks, LANES), f32),
            pltpu.VMEM((groups, fields, tiles, share, LANES), f32),
            pltpu.VMEM((groups, fields, tiles, share, LANES), f32),
            pltpu.VMEM((2, 4 * LANES, cells), jnp.bfloat16),
            pltpu.VMEM((fields, blocks, cells), f32),
            pltpu.VMEM((groups, fields * blocks, LANES), f32),
            pltpu.VMEM((E, fields * rows, LANES), f32),
            pltpu.VMEM((2, fields * rows, LANES), f32),
            pltpu.VMEM((1, fields * rows, LANES), f32),
            pltpu.VMEM((E, 2, fields, LANES), f32),
            pltpu.VMEM((E, 1, fields, LANES), f32),
            pltpu.VMEM((E, 2, fields, LANES), f32),
            pltpu.VMEM((E, 1, fields, LANES), f32),
            dma((5 + groups,)),
            dma((2,)),
            dma((groups, tiles)),
            dma((groups, tiles)),
            dma((4,)),
            dma((2, groups)),
            dma((2, groups)),
        ],
        compiler_params=pltpu.CompilerParams(
            collective_id=0, has_side_effects=True, vmem_limit_bytes=60 * 1024 * 1024
        ),
        cost_estimate=pl.CostEstimate(flops=20_000_000, bytes_accessed=2_000_000, transcendentals=0),
    )(
        jnp.transpose(old_fine, (1, 0, 2)),
        jnp.transpose(coarse_fine, (1, 0, 2)),
        old_owner,
        new_refine,
        parent_map,
        courant,
    )


def solution(mesh):
    in_specs = (
        P(("slab", "tile"), None, None),
        P(("slab", "tile"), None, None),
        P("slab", "tile", None),
        P("slab", "tile", None),
        P("slab", "tile", None),
        P(),
    )
    out_specs = P(None, "slab", "tile", None)
    body = functools.partial(local, mesh.shape["slab"], mesh.shape["tile"])
    return jax.shard_map(body, mesh=mesh, in_specs=in_specs, out_specs=out_specs, check_vma=False)
```

```python
import functools

import jax
import jax.numpy as jnp
from jax import lax
from jax.experimental import pallas as pl
from jax.experimental.pallas import tpu as pltpu
from jax.sharding import PartitionSpec as P

E = 8
BX = 16
BY = 4
LANES = 128
ORDER = (3, 0, 1, 2)
MESH = pl.DeviceIdType.MESH


def minmod(a, b):
    return jnp.maximum(jnp.minimum(a, jnp.maximum(b, 0.0)), jnp.minimum(b, 0.0))


def split(x):
    high = x.astype(jnp.bfloat16)
    low = (x - high.astype(jnp.float32)).astype(jnp.bfloat16)
    return high, low


def pick(onehot2, x):
    high, low = split(x)
    return jnp.dot(onehot2, jnp.concatenate([high, low], axis=0), preferred_element_type=jnp.float32)


def iota(shape, dim):
    return lax.broadcasted_iota(jnp.int32, shape, dim)


def column(row):
    size = row.shape[1]
    diag = iota((size, size), 0) == iota((size, size), 1)
    return jnp.sum(jnp.where(diag, jnp.broadcast_to(row, (size, size)), 0.0), axis=1, keepdims=True)


def twice(onehot):
    half = jnp.where(onehot, 1.0, 0.0).astype(jnp.bfloat16)
    return jnp.concatenate([half, half], axis=1)


def refine_matrix(h):
    rows, cols = 2 * 64, 512
    i, j = iota((rows, cols), 0), iota((rows, cols), 1)
    parent = ((j >> 7) << 4) + (((j >> 4) & 3) << 2) + ((j >> 1) & 3) + h * 64
    match = jnp.where(i == parent, 1.0, 0.0)
    out = [match]
    for bit in (6, 3, 0):
        sign = jnp.where(((j >> bit) & 1) == 1, 0.25, -0.25)
        out.append(match * sign)
    return jnp.concatenate([m.astype(jnp.bfloat16) for m in out], axis=0)


def parent_slopes(c):
    lane = iota(c.shape, 1)
    out = [c]
    for bit in (4, 2, 0):
        step = 1 << bit
        inside = ((lane >> bit) & 3) != 0
        below = jnp.where(inside, c - pltpu.roll(c, step, 1), 0.0)
        above = pltpu.roll(below, LANES - step, 1)
        out.append(minmod(below, above))
    return out


def swap_lanes(rows):
    lane = iota(rows[0].shape, 1)
    rows = list(rows)
    for b in range(4):
        step = 8 << b
        upper = ((lane >> (3 + b)) & 1) == 1
        for i in range(16):
            if i & (1 << b):
                continue
            j = i | (1 << b)
            x, y = rows[i], rows[j]
            rows[i] = jnp.where(upper, pltpu.roll(y, step, 1), x)
            rows[j] = jnp.where(upper, y, pltpu.roll(x, LANES - step, 1))
    return rows


def step_x(u, c):
    lane = iota(u.shape, 1)
    first, last = lane == 0, lane == LANES - 1
    d = u - jnp.where(first, 0.0, pltpu.roll(u, 1, 1))
    above = jnp.where(last, -u, pltpu.roll(d, LANES - 1, 1))
    g = u + 0.5 * minmod(d, above)
    return c * (g - jnp.where(first, 0.0, pltpu.roll(g, 1, 1)))


def step_y(u, c):
    n = u.shape[0]
    row = iota(u.shape, 0)
    d = u - pltpu.roll(u, 1, 0)
    g = u + 0.5 * minmod(d, pltpu.roll(d, n - 1, 0))
    return jnp.where((row >= 2) & (row <= n - 2), c * (g - pltpu.roll(g, 1, 0)), 0.0)


def kernel(
    slabs, tiles, old_hbm, coarse_hbm, owner_hbm, refine_hbm, parent_hbm, courant_hbm,
    out, owner_ref, refine_ref, parent_ref, courant, old, coarse, csend, crecv, send, recv, matrix, interp, tmp, region,
    zlow, zhigh, ysend_up, ysend_down, ylow, yhigh,
    load_sem, csem, asend, arecv, zsem, ysend_sem, yrecv_sem,
):
    slab, tile = lax.axis_index("slab"), lax.axis_index("tile")
    fields, blocks, cells = old.shape
    groups = cells // LANES
    rows = BY * E
    share = blocks // tiles
    up, down = lax.rem(slab + 1, slabs), lax.rem(slab + slabs - 1, slabs)
    has_down, has_up = slab > 0, slab < slabs - 1
    has_left, has_right = tile > 0, tile < tiles - 1

    barrier = pltpu.get_barrier_semaphore()
    for s in (up, down):
        pl.semaphore_signal(barrier, inc=1, device_id={"slab": s}, device_id_type=MESH)
    for o in range(1, tiles):
        pl.semaphore_signal(
            barrier, inc=1, device_id={"tile": lax.rem(tile + o, tiles)}, device_id_type=MESH
        )
    sources = (owner_hbm, refine_hbm, parent_hbm, courant_hbm, coarse_hbm)
    targets = (owner_ref, refine_ref, parent_ref, courant, coarse)
    loads = [pltpu.make_async_copy(a, b, load_sem.at[i]) for i, (a, b) in enumerate(zip(sources, targets))]
    for load in loads[::-1]:
        load.start()

    def load_old(g):
        at = pl.ds(g * LANES, LANES)
        return pltpu.make_async_copy(old_hbm.at[:, :, at], old.at[:, :, at], load_sem.at[5 + g])

    for g in ORDER:
        load_old(g).start()

    loads[4].wait()
    for f in range(fields):
        first = f // 2 * blocks
        if f % 2 or f + 1 < fields:
            csend[first:first + blocks, f % 2 * 64:f % 2 * 64 + 64] = coarse[f]
        else:
            csend[first:first + blocks // 2, :64] = coarse[f, :blocks // 2]
            csend[first:first + blocks // 2, 64:] = coarse[f, blocks // 2:]

    pl.semaphore_wait(barrier, tiles + 1)
    send_coarse = pltpu.make_async_remote_copy(
        csend, crecv, csem.at[0], csem.at[1], device_id={"slab": up}, device_id_type=MESH
    )
    send_coarse.start()

    for load in loads[:4]:
        load.wait()
    offset = owner_ref[0] - tile
    offset = jnp.where(offset < 0, offset + tiles, offset).astype(jnp.float32)
    square = (blocks, blocks)
    same = column(offset) == jnp.broadcast_to(offset, square)
    earlier = iota(square, 0) < iota(square, 1)
    rank = jnp.sum(jnp.where(same & earlier, 1.0, 0.0), axis=0, keepdims=True)
    place = offset * share + rank
    pack = twice(iota(square, 0).astype(jnp.float32) == jnp.broadcast_to(place, square))
    unpack_at = column(place) == iota(square, 1).astype(jnp.float32)
    refine = column(refine_ref[0].astype(jnp.float32)) > 0.5
    unpack = twice(unpack_at & ~refine)
    parents = twice((column(parent_ref[0].astype(jnp.float32)) == iota(square, 1).astype(jnp.float32)) & refine)

    def exchange(g, o):
        return pltpu.make_async_remote_copy(
            send.at[g, :, o], recv.at[g, :, o], asend.at[g, o], arecv.at[g, o],
            device_id={"tile": lax.rem(tile + o, tiles)}, device_id_type=MESH,
        )

    def send_group(g):
        for o in sorted(range(1, tiles), key=lambda o: -min(o, tiles - o)):
            exchange(g, o).start()

    def sent_group(g):
        for o in range(1, tiles):
            exchange(g, o).wait_send()

    for n, g in enumerate(ORDER):
        load_old(g).wait()
        for f in range(fields):
            packed = pick(pack, old[f, :, g * LANES:(g + 1) * LANES])
            send[g, f] = packed.reshape(tiles, share, LANES)
            recv[g, f, 0] = packed[:share]
        if n < 2:
            send_group(g)

    @pl.when(jnp.logical_not(has_down))
    def _():
        zlow[...] = jnp.zeros_like(zlow)

    @pl.when(jnp.logical_not(has_up))
    def _():
        zhigh[...] = jnp.zeros_like(zhigh)

    @pl.when(jnp.logical_not(has_left))
    def _():
        ylow[...] = jnp.zeros_like(ylow)

    @pl.when(jnp.logical_not(has_right))
    def _():
        yhigh[...] = jnp.zeros_like(yhigh)

    for h in range(2):
        matrix[h] = refine_matrix(h)
    sent_group(ORDER[0])
    send_group(ORDER[2])
    send_coarse.wait_recv()
    for p in range((fields + 1) // 2):
        first = p * blocks
        if 2 * p + 1 < fields:
            pair = crecv[first:first + blocks]
        else:
            pair = crecv[first:first + blocks // 2]
            pair = jnp.concatenate([pair, pltpu.roll(pair, 64, 1)], axis=0)
        parts = [split(part) for part in parent_slopes(pick(parents, pair))]
        high = jnp.concatenate([part[0] for part in parts], axis=1)
        low = jnp.concatenate([part[1] for part in parts], axis=1)
        for h in range(2):
            if 2 * p + h < fields:
                interp[2 * p + h] = jnp.dot(
                    high, matrix[h], preferred_element_type=jnp.float32
                ) + jnp.dot(low, matrix[h], preferred_element_type=jnp.float32)

    sent_group(ORDER[1])
    send_group(ORDER[3])
    send_up = pltpu.make_async_remote_copy(
        region.at[E - 2:E], zlow, zsem.at[0], zsem.at[1], device_id={"slab": up}, device_id_type=MESH
    )
    send_down = pltpu.make_async_remote_copy(
        region.at[0:1], zhigh, zsem.at[2], zsem.at[3], device_id={"slab": down}, device_id_type=MESH
    )

    def send_right(g):
        return pltpu.make_async_remote_copy(
            ysend_up.at[2 * g:2 * g + 2], ylow.at[2 * g:2 * g + 2], ysend_sem.at[0, g], yrecv_sem.at[0, g],
            device_id={"tile": lax.rem(tile + 1, tiles)}, device_id_type=MESH,
        )

    def send_left(g):
        return pltpu.make_async_remote_copy(
            ysend_down.at[2 * g:2 * g + 2], yhigh.at[2 * g:2 * g + 2], ysend_sem.at[1, g], yrecv_sem.at[1, g],
            device_id={"tile": lax.rem(tile + tiles - 1, tiles)}, device_id_type=MESH,
        )

    def at(f, z):
        return pl.ds(pl.multiple_of((f * E + z) * rows, rows), rows)

    def field_rows(f):
        return pl.ds(pl.multiple_of(f * rows, rows), rows)

    for g in ORDER:
        for o in range(1, tiles):
            exchange(g, o).wait_recv()
        for f in range(fields):
            moved = pick(unpack, recv[g, f].reshape(blocks, LANES))
            tmp[g, f * blocks:(f + 1) * blocks] = moved + interp[f, :, g * LANES:(g + 1) * LANES]
        turned = swap_lanes([tmp[g, pl.ds(b, fields * BY, stride=BX), :] for b in range(BX)])
        for j in range(BX):
            region[2 * g + j // E, pl.ds(j % E, fields * BY, stride=E), :] = turned[j]
        if g == 3:
            pl.when(has_up)(send_up.start)
        if g == 0:
            pl.when(has_down)(send_down.start)
        for z in (2 * g, 2 * g + 1):
            for i in range(2):
                ysend_up[z, i] = region[z, pl.ds(rows - 2 + i, fields, stride=rows), :]
            ysend_down[z, 0] = region[z, pl.ds(0, fields, stride=rows), :]
        pl.when(has_right)(send_right(g).start)
        pl.when(has_left)(send_left(g).start)

        def along_xy(f, carry, g=g):
            for z in (2 * g, 2 * g + 1):
                u = region[z, field_rows(f), :]
                out[at(f, z), :] = u - step_x(u, courant[2, f]) - step_y(u, courant[1, f])
            return carry

        lax.fori_loop(0, fields, along_xy, 0)

    def along_z(f, carry):
        c = courant[0, f]
        u = [region[z, field_rows(f), :] for z in range(E)]
        d = [None] + [u[z] - u[z - 1] for z in range(1, E)]
        g = [None] + [u[z] + 0.5 * minmod(d[z], d[z + 1]) for z in range(1, E - 1)]
        for z in range(2, E - 1):
            out[at(f, z), :] -= c * (g[z] - g[z - 1])
        return carry

    lax.fori_loop(0, fields, along_z, 0)

    for g in ORDER:
        pl.when(has_left)(send_right(g).wait_recv)
        pl.when(has_right)(send_left(g).wait_recv)

    number = iota((fields, LANES), 0)
    c = jnp.zeros((fields, LANES), jnp.float32)
    for f in range(fields):
        c = jnp.where(number == f, courant[1, f], c)

    def face(u, below, above):
        return u + 0.5 * minmod(below, above)

    for z in range(E):
        u = {y: region[z, pl.ds(y % rows, fields, stride=rows), :] for y in (0, 1, 2, -3, -2, -1)}
        low2, low1, high = ylow[z, 0], ylow[z, 1], yhigh[z, 0]
        d0, d1 = u[0] - low1, u[1] - u[0]
        g = {
            -1: face(low1, low1 - low2, d0),
            0: face(u[0], d0, d1),
            1: face(u[1], d1, u[2] - u[1]),
        }
        d = u[-1] - u[-2]
        g[rows - 2], g[rows - 1] = face(u[-2], u[-2] - u[-3], d), face(u[-1], d, high - u[-1])
        for y in (0, 1, rows - 1):
            out[pl.ds(z * rows + y, fields, stride=E * rows), :] -= c * (g[y] - g[y - 1])

    pl.when(has_down)(send_up.wait_recv)
    pl.when(has_up)(send_down.wait_recv)

    def edges(f, carry):
        c = courant[0, f]
        here = field_rows(f)
        u = {z: region[z, here, :] for z in (0, 1, 2, E - 3, E - 2, E - 1)}
        u[-2], u[-1], u[E] = zlow[0, here, :], zlow[1, here, :], zhigh[0, here, :]
        d = {z: u[z] - u[z - 1] for z in (-1, 0, 1, 2, E - 2, E - 1, E)}
        g = {z: u[z] + 0.5 * minmod(d[z], d[z + 1]) for z in (-1, 0, 1, E - 2, E - 1)}
        for z in (0, 1, E - 1):
            out[at(f, z), :] -= c * (g[z] - g[z - 1])
        return carry

    lax.fori_loop(0, fields, edges, 0)

    send_coarse.wait_send()
    sent_group(ORDER[2])
    sent_group(ORDER[3])
    for g in ORDER:
        pl.when(has_right)(send_right(g).wait_send)
        pl.when(has_left)(send_left(g).wait_send)
    pl.when(has_up)(send_up.wait_send)
    pl.when(has_down)(send_down.wait_send)


def local(slabs, tiles, old_fine, coarse_fine, old_owner, new_refine, parent_map, courant):
    blocks, fields, cells = old_fine.shape
    half = coarse_fine.shape[2]
    groups = cells // LANES
    share = blocks // tiles
    rows = BY * E
    f32 = jnp.float32
    vmem = pl.BlockSpec(memory_space=pltpu.VMEM)
    hbm = pl.BlockSpec(memory_space=pltpu.HBM)
    dma = pltpu.SemaphoreType.DMA
    operands = (
        jnp.transpose(old_fine, (1, 0, 2)),
        jnp.transpose(coarse_fine, (1, 0, 2)),
        old_owner,
        new_refine,
        parent_map,
        courant,
    )
    stepped = pl.pallas_call(
        functools.partial(kernel, slabs, tiles),
        out_shape=pltpu.VMEM((fields * E * rows, BX * E), f32),
        in_specs=[hbm] * 6,
        out_specs=vmem,
        scratch_shapes=[
            pltpu.VMEM(old_owner.shape, jnp.int32),
            pltpu.VMEM(new_refine.shape, jnp.int32),
            pltpu.VMEM(parent_map.shape, jnp.int32),
            pltpu.SMEM(courant.shape, f32),
            pltpu.VMEM((fields, blocks, cells), f32),
            pltpu.VMEM((fields, blocks, half), f32),
            pltpu.VMEM((fields * blocks // 2, LANES), f32),
            pltpu.VMEM((fields * blocks // 2, LANES), f32),
            pltpu.VMEM((groups, fields, tiles, share, LANES), f32),
            pltpu.VMEM((groups, fields, tiles, share, LANES), f32),
            pltpu.VMEM((2, 4 * LANES, cells), jnp.bfloat16),
            pltpu.VMEM((fields, blocks, cells), f32),
            pltpu.VMEM((groups, fields * blocks, LANES), f32),
            pltpu.VMEM((E, fields * rows, LANES), f32),
            pltpu.VMEM((2, fields * rows, LANES), f32),
            pltpu.VMEM((1, fields * rows, LANES), f32),
            pltpu.VMEM((E, 2, fields, LANES), f32),
            pltpu.VMEM((E, 1, fields, LANES), f32),
            pltpu.VMEM((E, 2, fields, LANES), f32),
            pltpu.VMEM((E, 1, fields, LANES), f32),
            dma((5 + groups,)),
            dma((2,)),
            dma((groups, tiles)),
            dma((groups, tiles)),
            dma((4,)),
            dma((2, groups)),
            dma((2, groups)),
        ],
        compiler_params=pltpu.CompilerParams(
            collective_id=0, has_side_effects=True, vmem_limit_bytes=32 * 1024 * 1024
        ),
        cost_estimate=pl.CostEstimate(flops=20_000_000, bytes_accessed=2_000_000, transcendentals=0),
    )(*(pltpu.with_memory_space_constraint(operand, pltpu.HBM) for operand in operands))
    return stepped.reshape(fields, E, rows, BX * E)


def solution(mesh):
    in_specs = (
        P(("slab", "tile"), None, None),
        P(("slab", "tile"), None, None),
        P("slab", "tile", None),
        P("slab", "tile", None),
        P("slab", "tile", None),
        P(),
    )
    out_specs = P(None, "slab", "tile", None)
    body = functools.partial(local, mesh.shape["slab"], mesh.shape["tile"])
    return jax.shard_map(body, mesh=mesh, in_specs=in_specs, out_specs=out_specs, check_vma=False)
```

```python
import functools

import jax
import jax.numpy as jnp
from jax import lax
from jax.experimental import pallas as pl
from jax.experimental.pallas import tpu as pltpu
from jax.sharding import PartitionSpec as P

E = 8
BX = 16
BY = 4
LANES = 128
ORDER = (3, 0, 1, 2)
MESH = pl.DeviceIdType.MESH


def minmod(a, b):
    return jnp.maximum(jnp.minimum(a, jnp.maximum(b, 0.0)), jnp.minimum(b, 0.0))


def split(x):
    high = x.astype(jnp.bfloat16)
    low = (x - high.astype(jnp.float32)).astype(jnp.bfloat16)
    return high, low


def pick(onehot2, x):
    high, low = split(x)
    return jnp.dot(onehot2, jnp.concatenate([high, low], axis=0), preferred_element_type=jnp.float32)


def iota(shape, dim):
    return lax.broadcasted_iota(jnp.int32, shape, dim)


def column(row):
    size = row.shape[1]
    diag = iota((size, size), 0) == iota((size, size), 1)
    return jnp.sum(jnp.where(diag, jnp.broadcast_to(row, (size, size)), 0.0), axis=1, keepdims=True)


def twice(onehot):
    half = jnp.where(onehot, 1.0, 0.0).astype(jnp.bfloat16)
    return jnp.concatenate([half, half], axis=1)


def refine_matrix(h):
    rows, cols = 2 * 64, 512
    i, j = iota((rows, cols), 0), iota((rows, cols), 1)
    parent = ((j >> 7) << 4) + (((j >> 4) & 3) << 2) + ((j >> 1) & 3) + h * 64
    match = jnp.where(i == parent, 1.0, 0.0)
    out = [match]
    for bit in (6, 3, 0):
        sign = jnp.where(((j >> bit) & 1) == 1, 0.25, -0.25)
        out.append(match * sign)
    return jnp.concatenate([m.astype(jnp.bfloat16) for m in out], axis=0)


def parent_slopes(c):
    lane = iota(c.shape, 1)
    out = [c]
    for bit in (4, 2, 0):
        step = 1 << bit
        inside = ((lane >> bit) & 3) != 0
        below = jnp.where(inside, c - pltpu.roll(c, step, 1), 0.0)
        above = pltpu.roll(below, LANES - step, 1)
        out.append(minmod(below, above))
    return out


def swap_lanes(rows):
    lane = iota(rows[0].shape, 1)
    rows = list(rows)
    for b in range(4):
        step = 8 << b
        upper = ((lane >> (3 + b)) & 1) == 1
        for i in range(16):
            if i & (1 << b):
                continue
            j = i | (1 << b)
            x, y = rows[i], rows[j]
            rows[i] = jnp.where(upper, pltpu.roll(y, step, 1), x)
            rows[j] = jnp.where(upper, y, pltpu.roll(x, LANES - step, 1))
    return rows


def step_x(u, c):
    lane = iota(u.shape, 1)
    first, last = lane == 0, lane == LANES - 1
    d = u - jnp.where(first, 0.0, pltpu.roll(u, 1, 1))
    above = jnp.where(last, -u, pltpu.roll(d, LANES - 1, 1))
    g = u + 0.5 * minmod(d, above)
    return c * (g - jnp.where(first, 0.0, pltpu.roll(g, 1, 1)))


def step_y(u, c):
    n = u.shape[0]
    row = iota(u.shape, 0)
    d = u - pltpu.roll(u, 1, 0)
    g = u + 0.5 * minmod(d, pltpu.roll(d, n - 1, 0))
    return jnp.where((row >= 2) & (row <= n - 2), c * (g - pltpu.roll(g, 1, 0)), 0.0)


def kernel(
    slabs, tiles, old_hbm, coarse_hbm, owner_hbm, refine_hbm, parent_hbm, courant_hbm,
    out, owner_ref, refine_ref, parent_ref, courant, old, coarse, csend, crecv, send, recv, matrix, interp, tmp, region,
    zlow, zhigh, ysend_up, ysend_down, ylow, yhigh,
    load_sem, csem, asend, arecv, zsem, ysend_sem, yrecv_sem,
):
    slab, tile = lax.axis_index("slab"), lax.axis_index("tile")
    fields, blocks, cells = old.shape
    groups = cells // LANES
    rows = BY * E
    share = blocks // tiles
    up, down = lax.rem(slab + 1, slabs), lax.rem(slab + slabs - 1, slabs)
    has_down, has_up = slab > 0, slab < slabs - 1
    has_left, has_right = tile > 0, tile < tiles - 1

    barrier = pltpu.get_barrier_semaphore()
    pl.semaphore_signal(barrier, inc=1, device_id={"slab": down}, device_id_type=MESH)

    @pl.when(has_up)
    def _():
        pl.semaphore_signal(barrier, inc=1, device_id={"slab": up}, device_id_type=MESH)

    for o in range(1, tiles):
        pl.semaphore_signal(
            barrier, inc=1, device_id={"tile": lax.rem(tile + o, tiles)}, device_id_type=MESH
        )
    sources = (owner_hbm, coarse_hbm, refine_hbm, parent_hbm, courant_hbm)
    targets = (owner_ref, coarse, refine_ref, parent_ref, courant)
    loads = [pltpu.make_async_copy(a, b, load_sem.at[i]) for i, (a, b) in enumerate(zip(sources, targets))]
    for load in loads:
        load.start()

    def load_old(g):
        at = pl.ds(g * LANES, LANES)
        return pltpu.make_async_copy(old_hbm.at[:, :, at], old.at[:, :, at], load_sem.at[5 + g])

    for g in ORDER:
        load_old(g).start()

    loads[0].wait()
    offset = owner_ref[0] - tile
    offset = jnp.where(offset < 0, offset + tiles, offset).astype(jnp.float32)
    square = (blocks, blocks)
    same = column(offset) == jnp.broadcast_to(offset, square)
    earlier = iota(square, 0) < iota(square, 1)
    rank = jnp.sum(jnp.where(same & earlier, 1.0, 0.0), axis=0, keepdims=True)
    place = offset * share + rank
    pack = twice(iota(square, 0).astype(jnp.float32) == jnp.broadcast_to(place, square))
    loads[1].wait()
    for f in range(fields):
        first = f // 2 * blocks
        if f % 2 or f + 1 < fields:
            csend[first:first + blocks, f % 2 * 64:f % 2 * 64 + 64] = coarse[f]
        else:
            csend[first:first + blocks // 2, :64] = coarse[f, :blocks // 2]
            csend[first:first + blocks // 2, 64:] = coarse[f, blocks // 2:]

    pl.semaphore_wait(barrier, tiles + jnp.minimum(slab, 1))

    send_coarse = pltpu.make_async_remote_copy(
        csend, crecv, csem.at[0], csem.at[1], device_id={"slab": up}, device_id_type=MESH
    )
    send_coarse.start()

    def exchange(g, o):
        return pltpu.make_async_remote_copy(
            send.at[g, :, o], recv.at[g, :, o], asend.at[g, o], arecv.at[g, o],
            device_id={"tile": lax.rem(tile + o, tiles)}, device_id_type=MESH,
        )

    def send_group(g):
        for o in sorted(range(1, tiles), key=lambda o: -min(o, tiles - o)):
            exchange(g, o).start()

    def sent_group(g):
        for o in range(1, tiles):
            exchange(g, o).wait_send()

    for n, g in enumerate(ORDER):
        load_old(g).wait()
        for f in range(fields):
            packed = pick(pack, old[f, :, g * LANES:(g + 1) * LANES])
            send[g, f] = packed.reshape(tiles, share, LANES)
            recv[g, f, 0] = packed[:share]
        if n < 2:
            send_group(g)

    @pl.when(jnp.logical_not(has_down))
    def _():
        zlow[...] = jnp.zeros_like(zlow)

    @pl.when(jnp.logical_not(has_up))
    def _():
        zhigh[...] = jnp.zeros_like(zhigh)

    @pl.when(jnp.logical_not(has_left))
    def _():
        ylow[...] = jnp.zeros_like(ylow)

    @pl.when(jnp.logical_not(has_right))
    def _():
        yhigh[...] = jnp.zeros_like(yhigh)

    for load in loads[2:]:
        load.wait()
    unpack_at = column(place) == iota(square, 1).astype(jnp.float32)
    refine = column(refine_ref[0].astype(jnp.float32)) > 0.5
    unpack = twice(unpack_at & ~refine)
    parents = twice((column(parent_ref[0].astype(jnp.float32)) == iota(square, 1).astype(jnp.float32)) & refine)
    for h in range(2):
        matrix[h] = refine_matrix(h)
    sent_group(ORDER[0])
    send_group(ORDER[2])
    send_coarse.wait_recv()
    for p in range((fields + 1) // 2):
        first = p * blocks
        if 2 * p + 1 < fields:
            pair = crecv[first:first + blocks]
        else:
            pair = crecv[first:first + blocks // 2]
            pair = jnp.concatenate([pair, pltpu.roll(pair, 64, 1)], axis=0)
        parts = [split(part) for part in parent_slopes(pick(parents, pair))]
        high = jnp.concatenate([part[0] for part in parts], axis=1)
        low = jnp.concatenate([part[1] for part in parts], axis=1)
        for h in range(2):
            if 2 * p + h < fields:
                interp[2 * p + h] = jnp.dot(
                    high, matrix[h], preferred_element_type=jnp.float32
                ) + jnp.dot(low, matrix[h], preferred_element_type=jnp.float32)

    sent_group(ORDER[1])
    send_group(ORDER[3])
    send_up = pltpu.make_async_remote_copy(
        region.at[E - 2:E], zlow, zsem.at[0], zsem.at[1], device_id={"slab": up}, device_id_type=MESH
    )
    send_down = pltpu.make_async_remote_copy(
        region.at[0:1], zhigh, zsem.at[2], zsem.at[3], device_id={"slab": down}, device_id_type=MESH
    )

    def send_right(g):
        return pltpu.make_async_remote_copy(
            ysend_up.at[2 * g:2 * g + 2], ylow.at[2 * g:2 * g + 2], ysend_sem.at[0, g], yrecv_sem.at[0, g],
            device_id={"tile": lax.rem(tile + 1, tiles)}, device_id_type=MESH,
        )

    def send_left(g):
        return pltpu.make_async_remote_copy(
            ysend_down.at[2 * g:2 * g + 2], yhigh.at[2 * g:2 * g + 2], ysend_sem.at[1, g], yrecv_sem.at[1, g],
            device_id={"tile": lax.rem(tile + tiles - 1, tiles)}, device_id_type=MESH,
        )

    def at(f, z):
        return pl.ds(pl.multiple_of((f * E + z) * rows, rows), rows)

    def field_rows(f):
        return pl.ds(pl.multiple_of(f * rows, rows), rows)

    for g in ORDER:
        for o in range(1, tiles):
            exchange(g, o).wait_recv()
        for f in range(fields):
            moved = pick(unpack, recv[g, f].reshape(blocks, LANES))
            tmp[g, f * blocks:(f + 1) * blocks] = moved + interp[f, :, g * LANES:(g + 1) * LANES]
        turned = swap_lanes([tmp[g, pl.ds(b, fields * BY, stride=BX), :] for b in range(BX)])
        for j in range(BX):
            region[2 * g + j // E, pl.ds(j % E, fields * BY, stride=E), :] = turned[j]
        if g == 3:
            pl.when(has_up)(send_up.start)
        if g == 0:
            pl.when(has_down)(send_down.start)
        for z in (2 * g, 2 * g + 1):
            for i in range(2):
                ysend_up[z, i] = region[z, pl.ds(rows - 2 + i, fields, stride=rows), :]
            ysend_down[z, 0] = region[z, pl.ds(0, fields, stride=rows), :]
        pl.when(has_right)(send_right(g).start)
        pl.when(has_left)(send_left(g).start)

        def along_xy(f, carry, g=g):
            for z in (2 * g, 2 * g + 1):
                u = region[z, field_rows(f), :]
                out[at(f, z), :] = u - step_x(u, courant[2, f]) - step_y(u, courant[1, f])
            return carry

        lax.fori_loop(0, fields, along_xy, 0)

    def along_z(f, carry):
        c = courant[0, f]
        u = [region[z, field_rows(f), :] for z in range(E)]
        d = [None] + [u[z] - u[z - 1] for z in range(1, E)]
        g = [None] + [u[z] + 0.5 * minmod(d[z], d[z + 1]) for z in range(1, E - 1)]
        for z in range(2, E - 1):
            out[at(f, z), :] -= c * (g[z] - g[z - 1])
        return carry

    lax.fori_loop(0, fields, along_z, 0)

    for g in ORDER:
        pl.when(has_left)(send_right(g).wait_recv)
        pl.when(has_right)(send_left(g).wait_recv)

    number = iota((fields, LANES), 0)
    c = jnp.zeros((fields, LANES), jnp.float32)
    for f in range(fields):
        c = jnp.where(number == f, courant[1, f], c)

    def face(u, below, above):
        return u + 0.5 * minmod(below, above)

    for z in range(E):
        u = {y: region[z, pl.ds(y % rows, fields, stride=rows), :] for y in (0, 1, 2, -3, -2, -1)}
        low2, low1, high = ylow[z, 0], ylow[z, 1], yhigh[z, 0]
        d0, d1 = u[0] - low1, u[1] - u[0]
        g = {
            -1: face(low1, low1 - low2, d0),
            0: face(u[0], d0, d1),
            1: face(u[1], d1, u[2] - u[1]),
        }
        d = u[-1] - u[-2]
        g[rows - 2], g[rows - 1] = face(u[-2], u[-2] - u[-3], d), face(u[-1], d, high - u[-1])
        for y in (0, 1, rows - 1):
            out[pl.ds(z * rows + y, fields, stride=E * rows), :] -= c * (g[y] - g[y - 1])

    pl.when(has_down)(send_up.wait_recv)
    pl.when(has_up)(send_down.wait_recv)

    def edges(f, carry):
        c = courant[0, f]
        here = field_rows(f)
        u = {z: region[z, here, :] for z in (0, 1, 2, E - 3, E - 2, E - 1)}
        u[-2], u[-1], u[E] = zlow[0, here, :], zlow[1, here, :], zhigh[0, here, :]
        d = {z: u[z] - u[z - 1] for z in (-1, 0, 1, 2, E - 2, E - 1, E)}
        g = {z: u[z] + 0.5 * minmod(d[z], d[z + 1]) for z in (-1, 0, 1, E - 2, E - 1)}
        for z in (0, 1, E - 1):
            out[at(f, z), :] -= c * (g[z] - g[z - 1])
        return carry

    lax.fori_loop(0, fields, edges, 0)

    send_coarse.wait_send()
    sent_group(ORDER[2])
    sent_group(ORDER[3])
    for g in ORDER:
        pl.when(has_right)(send_right(g).wait_send)
        pl.when(has_left)(send_left(g).wait_send)
    pl.when(has_up)(send_up.wait_send)
    pl.when(has_down)(send_down.wait_send)


def local(slabs, tiles, old_fine, coarse_fine, old_owner, new_refine, parent_map, courant):
    blocks, fields, cells = old_fine.shape
    half = coarse_fine.shape[2]
    groups = cells // LANES
    share = blocks // tiles
    rows = BY * E
    f32 = jnp.float32
    vmem = pl.BlockSpec(memory_space=pltpu.VMEM)
    hbm = pl.BlockSpec(memory_space=pltpu.HBM)
    dma = pltpu.SemaphoreType.DMA
    operands = (
        jnp.transpose(old_fine, (1, 0, 2)),
        jnp.transpose(coarse_fine, (1, 0, 2)),
        old_owner,
        new_refine,
        parent_map,
        courant,
    )
    stepped = pl.pallas_call(
        functools.partial(kernel, slabs, tiles),
        out_shape=pltpu.VMEM((fields * E * rows, BX * E), f32),
        in_specs=[hbm] * 6,
        out_specs=vmem,
        scratch_shapes=[
            pltpu.VMEM(old_owner.shape, jnp.int32),
            pltpu.VMEM(new_refine.shape, jnp.int32),
            pltpu.VMEM(parent_map.shape, jnp.int32),
            pltpu.SMEM(courant.shape, f32),
            pltpu.VMEM((fields, blocks, cells), f32),
            pltpu.VMEM((fields, blocks, half), f32),
            pltpu.VMEM((fields * blocks // 2, LANES), f32),
            pltpu.VMEM((fields * blocks // 2, LANES), f32),
            pltpu.VMEM((groups, fields, tiles, share, LANES), f32),
            pltpu.VMEM((groups, fields, tiles, share, LANES), f32),
            pltpu.VMEM((2, 4 * LANES, cells), jnp.bfloat16),
            pltpu.VMEM((fields, blocks, cells), f32),
            pltpu.VMEM((groups, fields * blocks, LANES), f32),
            pltpu.VMEM((E, fields * rows, LANES), f32),
            pltpu.VMEM((2, fields * rows, LANES), f32),
            pltpu.VMEM((1, fields * rows, LANES), f32),
            pltpu.VMEM((E, 2, fields, LANES), f32),
            pltpu.VMEM((E, 1, fields, LANES), f32),
            pltpu.VMEM((E, 2, fields, LANES), f32),
            pltpu.VMEM((E, 1, fields, LANES), f32),
            dma((5 + groups,)),
            dma((2,)),
            dma((groups, tiles)),
            dma((groups, tiles)),
            dma((4,)),
            dma((2, groups)),
            dma((2, groups)),
        ],
        compiler_params=pltpu.CompilerParams(
            collective_id=0, has_side_effects=True, vmem_limit_bytes=32 * 1024 * 1024
        ),
        cost_estimate=pl.CostEstimate(flops=20_000_000, bytes_accessed=2_000_000, transcendentals=0),
    )(*(pltpu.with_memory_space_constraint(operand, pltpu.HBM) for operand in operands))
    return stepped.reshape(fields, E, rows, BX * E)


def solution(mesh):
    in_specs = (
        P(("slab", "tile"), None, None),
        P(("slab", "tile"), None, None),
        P("slab", "tile", None),
        P("slab", "tile", None),
        P("slab", "tile", None),
        P(),
    )
    out_specs = P(None, "slab", "tile", None)
    body = functools.partial(local, mesh.shape["slab"], mesh.shape["tile"])
    return jax.shard_map(body, mesh=mesh, in_specs=in_specs, out_specs=out_specs, check_vma=False)
```

```python
import functools

import jax
import jax.numpy as jnp
from jax import lax
from jax.experimental import pallas as pl
from jax.experimental.pallas import tpu as pltpu
from jax.sharding import PartitionSpec as P

E = 8
BX = 16
BY = 4
LANES = 128
ORDER = (3, 0, 1, 2)
MESH = pl.DeviceIdType.MESH


def minmod(a, b):
    return jnp.maximum(jnp.minimum(a, jnp.maximum(b, 0.0)), jnp.minimum(b, 0.0))


def split(x):
    high = x.astype(jnp.bfloat16)
    low = (x - high.astype(jnp.float32)).astype(jnp.bfloat16)
    return high, low


def pick(onehot2, x):
    high, low = split(x)
    return jnp.dot(onehot2, jnp.concatenate([high, low], axis=0), preferred_element_type=jnp.float32)


def iota(shape, dim):
    return lax.broadcasted_iota(jnp.int32, shape, dim)


def column(row):
    size = row.shape[1]
    diag = iota((size, size), 0) == iota((size, size), 1)
    return jnp.sum(jnp.where(diag, jnp.broadcast_to(row, (size, size)), 0.0), axis=1, keepdims=True)


def twice(onehot):
    half = jnp.where(onehot, 1.0, 0.0).astype(jnp.bfloat16)
    return jnp.concatenate([half, half], axis=1)


def refine_matrix(h):
    rows, cols = 2 * 64, 512
    i, j = iota((rows, cols), 0), iota((rows, cols), 1)
    parent = ((j >> 7) << 4) + (((j >> 4) & 3) << 2) + ((j >> 1) & 3) + h * 64
    match = jnp.where(i == parent, 1.0, 0.0)
    out = [match]
    for bit in (6, 3, 0):
        sign = jnp.where(((j >> bit) & 1) == 1, 0.25, -0.25)
        out.append(match * sign)
    return jnp.concatenate([m.astype(jnp.bfloat16) for m in out], axis=0)


def parent_slopes(c):
    lane = iota(c.shape, 1)
    out = [c]
    for bit in (4, 2, 0):
        step = 1 << bit
        inside = ((lane >> bit) & 3) != 0
        below = jnp.where(inside, c - pltpu.roll(c, step, 1), 0.0)
        above = pltpu.roll(below, LANES - step, 1)
        out.append(minmod(below, above))
    return out


def swap_lanes(rows):
    lane = iota(rows[0].shape, 1)
    rows = list(rows)
    for b in range(4):
        step = 8 << b
        upper = ((lane >> (3 + b)) & 1) == 1
        for i in range(16):
            if i & (1 << b):
                continue
            j = i | (1 << b)
            x, y = rows[i], rows[j]
            rows[i] = jnp.where(upper, pltpu.roll(y, step, 1), x)
            rows[j] = jnp.where(upper, y, pltpu.roll(x, LANES - step, 1))
    return rows


def step_x(u, c):
    lane = iota(u.shape, 1)
    first, last = lane == 0, lane == LANES - 1
    d = u - jnp.where(first, 0.0, pltpu.roll(u, 1, 1))
    above = jnp.where(last, -u, pltpu.roll(d, LANES - 1, 1))
    g = u + 0.5 * minmod(d, above)
    return c * (g - jnp.where(first, 0.0, pltpu.roll(g, 1, 1)))


def step_y(u, c):
    n = u.shape[0]
    row = iota(u.shape, 0)
    d = u - pltpu.roll(u, 1, 0)
    g = u + 0.5 * minmod(d, pltpu.roll(d, n - 1, 0))
    return jnp.where((row >= 2) & (row <= n - 2), c * (g - pltpu.roll(g, 1, 0)), 0.0)


def kernel(
    slabs, tiles, old_hbm, coarse_hbm, owner_hbm, refine_hbm, parent_hbm, courant_hbm,
    out, owner_ref, refine_ref, parent_ref, courant, old, coarse, csend, crecv, send, recv, matrix, interp, tmp, region,
    zlow, zhigh, ysend_up, ysend_down, ylow, yhigh,
    load_sem, csem, asend, arecv, zsem, ysend_sem, yrecv_sem,
):
    slab, tile = lax.axis_index("slab"), lax.axis_index("tile")
    fields, blocks, cells = old.shape
    groups = cells // LANES
    rows = BY * E
    share = blocks // tiles
    up, down = lax.rem(slab + 1, slabs), lax.rem(slab + slabs - 1, slabs)
    has_down, has_up = slab > 0, slab < slabs - 1
    has_left, has_right = tile > 0, tile < tiles - 1

    barrier = pltpu.get_barrier_semaphore()
    pl.semaphore_signal(barrier, inc=1, device_id={"slab": down}, device_id_type=MESH)

    @pl.when(has_up)
    def _():
        pl.semaphore_signal(barrier, inc=1, device_id={"slab": up}, device_id_type=MESH)

    for o in range(1, tiles):
        pl.semaphore_signal(
            barrier, inc=1, device_id={"tile": lax.rem(tile + o, tiles)}, device_id_type=MESH
        )
    sources = (owner_hbm, coarse_hbm, refine_hbm, parent_hbm, courant_hbm)
    targets = (owner_ref, coarse, refine_ref, parent_ref, courant)
    loads = [pltpu.make_async_copy(a, b, load_sem.at[i]) for i, (a, b) in enumerate(zip(sources, targets))]
    for load in loads:
        load.start()

    def load_old(g):
        at = pl.ds(g * LANES, LANES)
        return pltpu.make_async_copy(old_hbm.at[:, :, at], old.at[:, :, at], load_sem.at[5 + g])

    for g in ORDER:
        load_old(g).start()

    loads[0].wait()
    offset = owner_ref[0] - tile
    offset = jnp.where(offset < 0, offset + tiles, offset).astype(jnp.float32)
    square = (blocks, blocks)
    same = column(offset) == jnp.broadcast_to(offset, square)
    earlier = iota(square, 0) < iota(square, 1)
    rank = jnp.sum(jnp.where(same & earlier, 1.0, 0.0), axis=0, keepdims=True)
    place = offset * share + rank
    pack = twice(iota(square, 0).astype(jnp.float32) == jnp.broadcast_to(place, square))
    loads[1].wait()
    for f in range(fields):
        first = f // 2 * blocks
        if f % 2 or f + 1 < fields:
            csend[first:first + blocks, f % 2 * 64:f % 2 * 64 + 64] = coarse[f]
        else:
            csend[first:first + blocks // 2, :64] = coarse[f, :blocks // 2]
            csend[first:first + blocks // 2, 64:] = coarse[f, blocks // 2:]

    pl.semaphore_wait(barrier, tiles + jnp.minimum(slab, 1))

    send_coarse = pltpu.make_async_remote_copy(
        csend, crecv, csem.at[0], csem.at[1], device_id={"slab": up}, device_id_type=MESH
    )
    send_coarse.start()

    def exchange(g, o):
        return pltpu.make_async_remote_copy(
            send.at[g, :, o], recv.at[g, :, o], asend.at[g, o], arecv.at[g, o],
            device_id={"tile": lax.rem(tile + o, tiles)}, device_id_type=MESH,
        )

    def send_group(g):
        for o in sorted(range(1, tiles), key=lambda o: -min(o, tiles - o)):
            exchange(g, o).start()

    def sent_group(g):
        for o in range(1, tiles):
            exchange(g, o).wait_send()

    for n, g in enumerate(ORDER):
        load_old(g).wait()
        for f in range(fields):
            packed = pick(pack, old[f, :, g * LANES:(g + 1) * LANES])
            send[g, f] = packed.reshape(tiles, share, LANES)
            recv[g, f, 0] = packed[:share]
        if n < 2:
            send_group(g)

    @pl.when(jnp.logical_not(has_down))
    def _():
        zlow[...] = jnp.zeros_like(zlow)

    @pl.when(jnp.logical_not(has_up))
    def _():
        zhigh[...] = jnp.zeros_like(zhigh)

    @pl.when(jnp.logical_not(has_left))
    def _():
        ylow[...] = jnp.zeros_like(ylow)

    @pl.when(jnp.logical_not(has_right))
    def _():
        yhigh[...] = jnp.zeros_like(yhigh)

    for load in loads[2:]:
        load.wait()
    unpack_at = column(place) == iota(square, 1).astype(jnp.float32)
    refine = column(refine_ref[0].astype(jnp.float32)) > 0.5
    unpack = twice(unpack_at & ~refine)
    parents = twice((column(parent_ref[0].astype(jnp.float32)) == iota(square, 1).astype(jnp.float32)) & refine)
    for h in range(2):
        matrix[h] = refine_matrix(h)
    sent_group(ORDER[0])
    send_group(ORDER[2])
    send_group(ORDER[3])
    send_coarse.wait_recv()
    for p in range((fields + 1) // 2):
        first = p * blocks
        if 2 * p + 1 < fields:
            pair = crecv[first:first + blocks]
        else:
            pair = crecv[first:first + blocks // 2]
            pair = jnp.concatenate([pair, pltpu.roll(pair, 64, 1)], axis=0)
        parts = [split(part) for part in parent_slopes(pick(parents, pair))]
        high = jnp.concatenate([part[0] for part in parts], axis=1)
        low = jnp.concatenate([part[1] for part in parts], axis=1)
        for h in range(2):
            if 2 * p + h < fields:
                interp[2 * p + h] = jnp.dot(
                    high, matrix[h], preferred_element_type=jnp.float32
                ) + jnp.dot(low, matrix[h], preferred_element_type=jnp.float32)

    send_up = pltpu.make_async_remote_copy(
        region.at[E - 2:E], zlow, zsem.at[0], zsem.at[1], device_id={"slab": up}, device_id_type=MESH
    )
    send_down = pltpu.make_async_remote_copy(
        region.at[0:1], zhigh, zsem.at[2], zsem.at[3], device_id={"slab": down}, device_id_type=MESH
    )

    def send_right(g):
        return pltpu.make_async_remote_copy(
            ysend_up.at[2 * g:2 * g + 2], ylow.at[2 * g:2 * g + 2], ysend_sem.at[0, g], yrecv_sem.at[0, g],
            device_id={"tile": lax.rem(tile + 1, tiles)}, device_id_type=MESH,
        )

    def send_left(g):
        return pltpu.make_async_remote_copy(
            ysend_down.at[2 * g:2 * g + 2], yhigh.at[2 * g:2 * g + 2], ysend_sem.at[1, g], yrecv_sem.at[1, g],
            device_id={"tile": lax.rem(tile + tiles - 1, tiles)}, device_id_type=MESH,
        )

    def at(f, z):
        return pl.ds(pl.multiple_of((f * E + z) * rows, rows), rows)

    def field_rows(f):
        return pl.ds(pl.multiple_of(f * rows, rows), rows)

    for g in ORDER:
        for o in range(1, tiles):
            exchange(g, o).wait_recv()
        for f in range(fields):
            moved = pick(unpack, recv[g, f].reshape(blocks, LANES))
            tmp[g, f * blocks:(f + 1) * blocks] = moved + interp[f, :, g * LANES:(g + 1) * LANES]
        turned = swap_lanes([tmp[g, pl.ds(b, fields * BY, stride=BX), :] for b in range(BX)])
        for j in range(BX):
            region[2 * g + j // E, pl.ds(j % E, fields * BY, stride=E), :] = turned[j]
        if g == 3:
            pl.when(has_up)(send_up.start)
        if g == 0:
            pl.when(has_down)(send_down.start)
        for z in (2 * g, 2 * g + 1):
            for i in range(2):
                ysend_up[z, i] = region[z, pl.ds(rows - 2 + i, fields, stride=rows), :]
            ysend_down[z, 0] = region[z, pl.ds(0, fields, stride=rows), :]
        pl.when(has_right)(send_right(g).start)
        pl.when(has_left)(send_left(g).start)

        def along_xy(f, carry, g=g):
            for z in (2 * g, 2 * g + 1):
                u = region[z, field_rows(f), :]
                out[at(f, z), :] = u - step_x(u, courant[2, f]) - step_y(u, courant[1, f])
            return carry

        lax.fori_loop(0, fields, along_xy, 0, unroll=True)

    def along_z(f, carry):
        c = courant[0, f]
        u = [region[z, field_rows(f), :] for z in range(E)]
        d = [None] + [u[z] - u[z - 1] for z in range(1, E)]
        g = [None] + [u[z] + 0.5 * minmod(d[z], d[z + 1]) for z in range(1, E - 1)]
        for z in range(2, E - 1):
            out[at(f, z), :] -= c * (g[z] - g[z - 1])
        return carry

    lax.fori_loop(0, fields, along_z, 0, unroll=True)

    for g in ORDER:
        pl.when(has_left)(send_right(g).wait_recv)
        pl.when(has_right)(send_left(g).wait_recv)

    number = iota((fields, LANES), 0)
    c = jnp.zeros((fields, LANES), jnp.float32)
    for f in range(fields):
        c = jnp.where(number == f, courant[1, f], c)

    def face(u, below, above):
        return u + 0.5 * minmod(below, above)

    for z in range(E):
        u = {y: region[z, pl.ds(y % rows, fields, stride=rows), :] for y in (0, 1, 2, -3, -2, -1)}
        low2, low1, high = ylow[z, 0], ylow[z, 1], yhigh[z, 0]
        d0, d1 = u[0] - low1, u[1] - u[0]
        g = {
            -1: face(low1, low1 - low2, d0),
            0: face(u[0], d0, d1),
            1: face(u[1], d1, u[2] - u[1]),
        }
        d = u[-1] - u[-2]
        g[rows - 2], g[rows - 1] = face(u[-2], u[-2] - u[-3], d), face(u[-1], d, high - u[-1])
        for y in (0, 1, rows - 1):
            out[pl.ds(z * rows + y, fields, stride=E * rows), :] -= c * (g[y] - g[y - 1])

    pl.when(has_down)(send_up.wait_recv)
    pl.when(has_up)(send_down.wait_recv)

    def edges(f, carry):
        c = courant[0, f]
        here = field_rows(f)
        u = {z: region[z, here, :] for z in (0, 1, 2, E - 3, E - 2, E - 1)}
        u[-2], u[-1], u[E] = zlow[0, here, :], zlow[1, here, :], zhigh[0, here, :]
        d = {z: u[z] - u[z - 1] for z in (-1, 0, 1, 2, E - 2, E - 1, E)}
        g = {z: u[z] + 0.5 * minmod(d[z], d[z + 1]) for z in (-1, 0, 1, E - 2, E - 1)}
        for z in (0, 1, E - 1):
            out[at(f, z), :] -= c * (g[z] - g[z - 1])
        return carry

    lax.fori_loop(0, fields, edges, 0, unroll=True)

    send_coarse.wait_send()
    for g in ORDER[1:]:
        sent_group(g)
    for g in ORDER:
        pl.when(has_right)(send_right(g).wait_send)
        pl.when(has_left)(send_left(g).wait_send)
    pl.when(has_up)(send_up.wait_send)
    pl.when(has_down)(send_down.wait_send)


def local(slabs, tiles, old_fine, coarse_fine, old_owner, new_refine, parent_map, courant):
    blocks, fields, cells = old_fine.shape
    half = coarse_fine.shape[2]
    groups = cells // LANES
    share = blocks // tiles
    rows = BY * E
    f32 = jnp.float32
    vmem = pl.BlockSpec(memory_space=pltpu.VMEM)
    hbm = pl.BlockSpec(memory_space=pltpu.HBM)
    dma = pltpu.SemaphoreType.DMA
    operands = (
        jnp.transpose(old_fine, (1, 0, 2)),
        jnp.transpose(coarse_fine, (1, 0, 2)),
        old_owner,
        new_refine,
        parent_map,
        courant,
    )
    stepped = pl.pallas_call(
        functools.partial(kernel, slabs, tiles),
        out_shape=pltpu.VMEM((fields * E * rows, BX * E), f32),
        in_specs=[hbm] * 6,
        out_specs=vmem,
        scratch_shapes=[
            pltpu.VMEM(old_owner.shape, jnp.int32),
            pltpu.VMEM(new_refine.shape, jnp.int32),
            pltpu.VMEM(parent_map.shape, jnp.int32),
            pltpu.SMEM(courant.shape, f32),
            pltpu.VMEM((fields, blocks, cells), f32),
            pltpu.VMEM((fields, blocks, half), f32),
            pltpu.VMEM((fields * blocks // 2, LANES), f32),
            pltpu.VMEM((fields * blocks // 2, LANES), f32),
            pltpu.VMEM((groups, fields, tiles, share, LANES), f32),
            pltpu.VMEM((groups, fields, tiles, share, LANES), f32),
            pltpu.VMEM((2, 4 * LANES, cells), jnp.bfloat16),
            pltpu.VMEM((fields, blocks, cells), f32),
            pltpu.VMEM((groups, fields * blocks, LANES), f32),
            pltpu.VMEM((E, fields * rows, LANES), f32),
            pltpu.VMEM((2, fields * rows, LANES), f32),
            pltpu.VMEM((1, fields * rows, LANES), f32),
            pltpu.VMEM((E, 2, fields, LANES), f32),
            pltpu.VMEM((E, 1, fields, LANES), f32),
            pltpu.VMEM((E, 2, fields, LANES), f32),
            pltpu.VMEM((E, 1, fields, LANES), f32),
            dma((5 + groups,)),
            dma((2,)),
            dma((groups, tiles)),
            dma((groups, tiles)),
            dma((4,)),
            dma((2, groups)),
            dma((2, groups)),
        ],
        compiler_params=pltpu.CompilerParams(
            collective_id=0, has_side_effects=True, vmem_limit_bytes=32 * 1024 * 1024
        ),
        cost_estimate=pl.CostEstimate(flops=20_000_000, bytes_accessed=2_000_000, transcendentals=0),
    )(*(pltpu.with_memory_space_constraint(operand, pltpu.HBM) for operand in operands))
    return stepped.reshape(fields, E, rows, BX * E)


def solution(mesh):
    in_specs = (
        P(("slab", "tile"), None, None),
        P(("slab", "tile"), None, None),
        P("slab", "tile", None),
        P("slab", "tile", None),
        P("slab", "tile", None),
        P(),
    )
    out_specs = P(None, "slab", "tile", None)
    body = functools.partial(local, mesh.shape["slab"], mesh.shape["tile"])
    return jax.shard_map(body, mesh=mesh, in_specs=in_specs, out_specs=out_specs, check_vma=False)
```

```python
import functools

import jax
import jax.numpy as jnp
from jax import lax
from jax.experimental import pallas as pl
from jax.experimental.pallas import tpu as pltpu
from jax.sharding import PartitionSpec as P

E = 8
BX = 16
BY = 4
LANES = 128
ORDER = (3, 0, 1, 2)
MESH = pl.DeviceIdType.MESH


def minmod(a, b):
    return jnp.maximum(jnp.minimum(a, jnp.maximum(b, 0.0)), jnp.minimum(b, 0.0))


def split(x):
    high = x.astype(jnp.bfloat16)
    low = (x - high.astype(jnp.float32)).astype(jnp.bfloat16)
    return high, low


def pick(onehot2, x):
    high, low = split(x)
    return jnp.dot(onehot2, jnp.concatenate([high, low], axis=0), preferred_element_type=jnp.float32)


def iota(shape, dim):
    return lax.broadcasted_iota(jnp.int32, shape, dim)


def column(row):
    size = row.shape[1]
    diag = iota((size, size), 0) == iota((size, size), 1)
    return jnp.sum(jnp.where(diag, jnp.broadcast_to(row, (size, size)), 0.0), axis=1, keepdims=True)


def twice(onehot):
    half = jnp.where(onehot, 1.0, 0.0).astype(jnp.bfloat16)
    return jnp.concatenate([half, half], axis=1)


def refine_matrix(h):
    rows, cols = 2 * 64, 512
    i, j = iota((rows, cols), 0), iota((rows, cols), 1)
    parent = ((j >> 7) << 4) + (((j >> 4) & 3) << 2) + ((j >> 1) & 3) + h * 64
    match = jnp.where(i == parent, 1.0, 0.0)
    out = [match]
    for bit in (6, 3, 0):
        sign = jnp.where(((j >> bit) & 1) == 1, 0.25, -0.25)
        out.append(match * sign)
    return jnp.concatenate([m.astype(jnp.bfloat16) for m in out], axis=0)


def parent_slopes(c):
    lane = iota(c.shape, 1)
    out = [c]
    for bit in (4, 2, 0):
        step = 1 << bit
        inside = ((lane >> bit) & 3) != 0
        below = jnp.where(inside, c - pltpu.roll(c, step, 1), 0.0)
        above = pltpu.roll(below, LANES - step, 1)
        out.append(minmod(below, above))
    return out


def swap_lanes(rows):
    lane = iota(rows[0].shape, 1)
    rows = list(rows)
    for b in range(4):
        step = 8 << b
        upper = ((lane >> (3 + b)) & 1) == 1
        for i in range(16):
            if i & (1 << b):
                continue
            j = i | (1 << b)
            x, y = rows[i], rows[j]
            rows[i] = jnp.where(upper, pltpu.roll(y, step, 1), x)
            rows[j] = jnp.where(upper, y, pltpu.roll(x, LANES - step, 1))
    return rows


def step_x(u, c):
    lane = iota(u.shape, 1)
    first, last = lane == 0, lane == LANES - 1
    d = u - jnp.where(first, 0.0, pltpu.roll(u, 1, 1))
    above = jnp.where(last, -u, pltpu.roll(d, LANES - 1, 1))
    g = u + 0.5 * minmod(d, above)
    return c * (g - jnp.where(first, 0.0, pltpu.roll(g, 1, 1)))


def step_y(u, c):
    n = u.shape[0]
    row = iota(u.shape, 0)
    d = u - pltpu.roll(u, 1, 0)
    g = u + 0.5 * minmod(d, pltpu.roll(d, n - 1, 0))
    return jnp.where((row >= 2) & (row <= n - 2), c * (g - pltpu.roll(g, 1, 0)), 0.0)


def kernel(
    slabs, tiles, old_hbm, coarse_hbm, owner_hbm, refine_hbm, parent_hbm, courant_hbm,
    out, owner_ref, refine_ref, parent_ref, courant, old, coarse, csend, crecv, send, recv, matrix, stacked, interp, tmp, region,
    zlow, zhigh, ysend_up, ysend_down, ylow, yhigh,
    load_sem, csem, asend, arecv, zsem, ysend_sem, yrecv_sem,
):
    slab, tile = lax.axis_index("slab"), lax.axis_index("tile")
    fields, blocks, cells = old.shape
    groups = cells // LANES
    rows = BY * E
    share = blocks // tiles
    up, down = lax.rem(slab + 1, slabs), lax.rem(slab + slabs - 1, slabs)
    has_down, has_up = slab > 0, slab < slabs - 1
    has_left, has_right = tile > 0, tile < tiles - 1

    barrier = pltpu.get_barrier_semaphore()
    pl.semaphore_signal(barrier, inc=1, device_id={"slab": down}, device_id_type=MESH)

    @pl.when(has_up)
    def _():
        pl.semaphore_signal(barrier, inc=1, device_id={"slab": up}, device_id_type=MESH)

    for o in range(1, tiles):
        pl.semaphore_signal(
            barrier, inc=1, device_id={"tile": lax.rem(tile + o, tiles)}, device_id_type=MESH
        )
    sources = (owner_hbm, coarse_hbm, refine_hbm, parent_hbm, courant_hbm)
    targets = (owner_ref, coarse, refine_ref, parent_ref, courant)
    loads = [pltpu.make_async_copy(a, b, load_sem.at[i]) for i, (a, b) in enumerate(zip(sources, targets))]
    for load in loads:
        load.start()

    def load_old(g):
        at = pl.ds(g * LANES, LANES)
        return pltpu.make_async_copy(old_hbm.at[:, :, at], old.at[:, :, at], load_sem.at[5 + g])

    for g in ORDER:
        load_old(g).start()

    loads[0].wait()
    offset = owner_ref[0] - tile
    offset = jnp.where(offset < 0, offset + tiles, offset).astype(jnp.float32)
    square = (blocks, blocks)
    same = column(offset) == jnp.broadcast_to(offset, square)
    earlier = iota(square, 0) < iota(square, 1)
    rank = jnp.sum(jnp.where(same & earlier, 1.0, 0.0), axis=0, keepdims=True)
    place = offset * share + rank
    pack = twice(iota(square, 0).astype(jnp.float32) == jnp.broadcast_to(place, square))
    loads[1].wait()
    for f in range(fields):
        first = f // 2 * blocks
        if f % 2 or f + 1 < fields:
            csend[first:first + blocks, f % 2 * 64:f % 2 * 64 + 64] = coarse[f]
        else:
            csend[first:first + blocks // 2, :64] = coarse[f, :blocks // 2]
            csend[first:first + blocks // 2, 64:] = coarse[f, blocks // 2:]

    pl.semaphore_wait(barrier, tiles + jnp.minimum(slab, 1))

    send_coarse = pltpu.make_async_remote_copy(
        csend, crecv, csem.at[0], csem.at[1], device_id={"slab": up}, device_id_type=MESH
    )
    send_coarse.start()

    def exchange(g, o):
        return pltpu.make_async_remote_copy(
            send.at[g, :, o], recv.at[g, :, o], asend.at[g, o], arecv.at[g, o],
            device_id={"tile": lax.rem(tile + o, tiles)}, device_id_type=MESH,
        )

    def send_group(g):
        for o in sorted(range(1, tiles), key=lambda o: -min(o, tiles - o)):
            exchange(g, o).start()

    def sent_group(g):
        for o in range(1, tiles):
            exchange(g, o).wait_send()

    for n, g in enumerate(ORDER):
        load_old(g).wait()
        for f in range(fields):
            packed = pick(pack, old[f, :, g * LANES:(g + 1) * LANES])
            send[g, f] = packed.reshape(tiles, share, LANES)
            recv[g, f, 0] = packed[:share]
        if n < 2:
            send_group(g)

    @pl.when(jnp.logical_not(has_down))
    def _():
        zlow[...] = jnp.zeros_like(zlow)

    @pl.when(jnp.logical_not(has_up))
    def _():
        zhigh[...] = jnp.zeros_like(zhigh)

    @pl.when(jnp.logical_not(has_left))
    def _():
        ylow[...] = jnp.zeros_like(ylow)

    @pl.when(jnp.logical_not(has_right))
    def _():
        yhigh[...] = jnp.zeros_like(yhigh)

    for load in loads[2:]:
        load.wait()
    unpack_at = column(place) == iota(square, 1).astype(jnp.float32)
    refine = column(refine_ref[0].astype(jnp.float32)) > 0.5
    unpack = twice(unpack_at & ~refine)
    parents = twice((column(parent_ref[0].astype(jnp.float32)) == iota(square, 1).astype(jnp.float32)) & refine)
    for h in range(2):
        matrix[h] = refine_matrix(h)
    sent_group(ORDER[0])
    send_group(ORDER[2])
    send_group(ORDER[3])
    send_coarse.wait_recv()
    for p in range((fields + 1) // 2):
        first = p * blocks
        if 2 * p + 1 < fields:
            pair = crecv[first:first + blocks]
        else:
            pair = crecv[first:first + blocks // 2]
            pair = jnp.concatenate([pair, pltpu.roll(pair, 64, 1)], axis=0)
        parts = [split(part) for part in parent_slopes(pick(parents, pair))]
        for n in range(2):
            part = jnp.concatenate([part[n] for part in parts], axis=1)
            at = (2 * p + n) * blocks
            stacked[at:at + blocks] = part

    def refined(g):
        columns = slice(g * LANES, (g + 1) * LANES)
        for h in range(2):
            count = (fields + 1 - h) // 2
            both = jnp.dot(
                stacked[:2 * count * blocks], matrix[h, :, columns], preferred_element_type=jnp.float32
            )
            for p in range(count):
                at = 2 * p * blocks
                interp[g, 2 * p + h] = both[at:at + blocks] + both[at + blocks:at + 2 * blocks]

    send_up = pltpu.make_async_remote_copy(
        region.at[E - 2:E], zlow, zsem.at[0], zsem.at[1], device_id={"slab": up}, device_id_type=MESH
    )
    send_down = pltpu.make_async_remote_copy(
        region.at[0:1], zhigh, zsem.at[2], zsem.at[3], device_id={"slab": down}, device_id_type=MESH
    )

    def send_right(g):
        return pltpu.make_async_remote_copy(
            ysend_up.at[2 * g:2 * g + 2], ylow.at[2 * g:2 * g + 2], ysend_sem.at[0, g], yrecv_sem.at[0, g],
            device_id={"tile": lax.rem(tile + 1, tiles)}, device_id_type=MESH,
        )

    def send_left(g):
        return pltpu.make_async_remote_copy(
            ysend_down.at[2 * g:2 * g + 2], yhigh.at[2 * g:2 * g + 2], ysend_sem.at[1, g], yrecv_sem.at[1, g],
            device_id={"tile": lax.rem(tile + tiles - 1, tiles)}, device_id_type=MESH,
        )

    def at(f, z):
        return pl.ds(pl.multiple_of((f * E + z) * rows, rows), rows)

    def field_rows(f):
        return pl.ds(pl.multiple_of(f * rows, rows), rows)

    for g in ORDER:
        refined(g)
        for o in range(1, tiles):
            exchange(g, o).wait_recv()
        for f in range(fields):
            moved = pick(unpack, recv[g, f].reshape(blocks, LANES))
            tmp[g, f * blocks:(f + 1) * blocks] = moved + interp[g, f]
        turned = swap_lanes([tmp[g, pl.ds(b, fields * BY, stride=BX), :] for b in range(BX)])
        for j in range(BX):
            region[2 * g + j // E, pl.ds(j % E, fields * BY, stride=E), :] = turned[j]
        if g == 3:
            pl.when(has_up)(send_up.start)
        if g == 0:
            pl.when(has_down)(send_down.start)
        for z in (2 * g, 2 * g + 1):
            for i in range(2):
                ysend_up[z, i] = region[z, pl.ds(rows - 2 + i, fields, stride=rows), :]
            ysend_down[z, 0] = region[z, pl.ds(0, fields, stride=rows), :]
        pl.when(has_right)(send_right(g).start)
        pl.when(has_left)(send_left(g).start)

        def along_xy(f, carry, g=g):
            for z in (2 * g, 2 * g + 1):
                u = region[z, field_rows(f), :]
                out[at(f, z), :] = u - step_x(u, courant[2, f]) - step_y(u, courant[1, f])
            return carry

        lax.fori_loop(0, fields, along_xy, 0, unroll=True)

    def along_z(f, carry):
        c = courant[0, f]
        u = [region[z, field_rows(f), :] for z in range(E)]
        d = [None] + [u[z] - u[z - 1] for z in range(1, E)]
        g = [None] + [u[z] + 0.5 * minmod(d[z], d[z + 1]) for z in range(1, E - 1)]
        for z in range(2, E - 1):
            out[at(f, z), :] -= c * (g[z] - g[z - 1])
        return carry

    lax.fori_loop(0, fields, along_z, 0, unroll=True)

    for g in ORDER:
        pl.when(has_left)(send_right(g).wait_recv)
        pl.when(has_right)(send_left(g).wait_recv)

    number = iota((fields, LANES), 0)
    c = jnp.zeros((fields, LANES), jnp.float32)
    for f in range(fields):
        c = jnp.where(number == f, courant[1, f], c)

    def face(u, below, above):
        return u + 0.5 * minmod(below, above)

    for z in range(E):
        u = {y: region[z, pl.ds(y % rows, fields, stride=rows), :] for y in (0, 1, 2, -3, -2, -1)}
        low2, low1, high = ylow[z, 0], ylow[z, 1], yhigh[z, 0]
        d0, d1 = u[0] - low1, u[1] - u[0]
        g = {
            -1: face(low1, low1 - low2, d0),
            0: face(u[0], d0, d1),
            1: face(u[1], d1, u[2] - u[1]),
        }
        d = u[-1] - u[-2]
        g[rows - 2], g[rows - 1] = face(u[-2], u[-2] - u[-3], d), face(u[-1], d, high - u[-1])
        for y in (0, 1, rows - 1):
            out[pl.ds(z * rows + y, fields, stride=E * rows), :] -= c * (g[y] - g[y - 1])

    pl.when(has_down)(send_up.wait_recv)
    pl.when(has_up)(send_down.wait_recv)

    def edges(f, carry):
        c = courant[0, f]
        here = field_rows(f)
        u = {z: region[z, here, :] for z in (0, 1, 2, E - 3, E - 2, E - 1)}
        u[-2], u[-1], u[E] = zlow[0, here, :], zlow[1, here, :], zhigh[0, here, :]
        d = {z: u[z] - u[z - 1] for z in (-1, 0, 1, 2, E - 2, E - 1, E)}
        g = {z: u[z] + 0.5 * minmod(d[z], d[z + 1]) for z in (-1, 0, 1, E - 2, E - 1)}
        for z in (0, 1, E - 1):
            out[at(f, z), :] -= c * (g[z] - g[z - 1])
        return carry

    lax.fori_loop(0, fields, edges, 0, unroll=True)

    send_coarse.wait_send()
    for g in ORDER[1:]:
        sent_group(g)
    for g in ORDER:
        pl.when(has_right)(send_right(g).wait_send)
        pl.when(has_left)(send_left(g).wait_send)
    pl.when(has_up)(send_up.wait_send)
    pl.when(has_down)(send_down.wait_send)


def local(slabs, tiles, old_fine, coarse_fine, old_owner, new_refine, parent_map, courant):
    blocks, fields, cells = old_fine.shape
    half = coarse_fine.shape[2]
    groups = cells // LANES
    share = blocks // tiles
    rows = BY * E
    f32 = jnp.float32
    vmem = pl.BlockSpec(memory_space=pltpu.VMEM)
    hbm = pl.BlockSpec(memory_space=pltpu.HBM)
    dma = pltpu.SemaphoreType.DMA
    operands = (
        jnp.transpose(old_fine, (1, 0, 2)),
        jnp.transpose(coarse_fine, (1, 0, 2)),
        old_owner,
        new_refine,
        parent_map,
        courant,
    )
    stepped = pl.pallas_call(
        functools.partial(kernel, slabs, tiles),
        out_shape=pltpu.VMEM((fields * E * rows, BX * E), f32),
        in_specs=[hbm] * 6,
        out_specs=vmem,
        scratch_shapes=[
            pltpu.VMEM(old_owner.shape, jnp.int32),
            pltpu.VMEM(new_refine.shape, jnp.int32),
            pltpu.VMEM(parent_map.shape, jnp.int32),
            pltpu.SMEM(courant.shape, f32),
            pltpu.VMEM((fields, blocks, cells), f32),
            pltpu.VMEM((fields, blocks, half), f32),
            pltpu.VMEM((fields * blocks // 2, LANES), f32),
            pltpu.VMEM((fields * blocks // 2, LANES), f32),
            pltpu.VMEM((groups, fields, tiles, share, LANES), f32),
            pltpu.VMEM((groups, fields, tiles, share, LANES), f32),
            pltpu.VMEM((2, 4 * LANES, cells), jnp.bfloat16),
            pltpu.VMEM(((fields + 1) // 2 * 2 * blocks, 4 * LANES), jnp.bfloat16),
            pltpu.VMEM((groups, fields, blocks, LANES), f32),
            pltpu.VMEM((groups, fields * blocks, LANES), f32),
            pltpu.VMEM((E, fields * rows, LANES), f32),
            pltpu.VMEM((2, fields * rows, LANES), f32),
            pltpu.VMEM((1, fields * rows, LANES), f32),
            pltpu.VMEM((E, 2, fields, LANES), f32),
            pltpu.VMEM((E, 1, fields, LANES), f32),
            pltpu.VMEM((E, 2, fields, LANES), f32),
            pltpu.VMEM((E, 1, fields, LANES), f32),
            dma((5 + groups,)),
            dma((2,)),
            dma((groups, tiles)),
            dma((groups, tiles)),
            dma((4,)),
            dma((2, groups)),
            dma((2, groups)),
        ],
        compiler_params=pltpu.CompilerParams(
            collective_id=0, has_side_effects=True, vmem_limit_bytes=32 * 1024 * 1024
        ),
        cost_estimate=pl.CostEstimate(flops=20_000_000, bytes_accessed=2_000_000, transcendentals=0),
    )(*(pltpu.with_memory_space_constraint(operand, pltpu.HBM) for operand in operands))
    return stepped.reshape(fields, E, rows, BX * E)


def solution(mesh):
    in_specs = (
        P(("slab", "tile"), None, None),
        P(("slab", "tile"), None, None),
        P("slab", "tile", None),
        P("slab", "tile", None),
        P("slab", "tile", None),
        P(),
    )
    out_specs = P(None, "slab", "tile", None)
    body = functools.partial(local, mesh.shape["slab"], mesh.shape["tile"])
    return jax.shard_map(body, mesh=mesh, in_specs=in_specs, out_specs=out_specs, check_vma=False)
```

```python
import functools

import jax
import jax.numpy as jnp
from jax import lax
from jax.experimental import pallas as pl
from jax.experimental.pallas import tpu as pltpu
from jax.sharding import PartitionSpec as P

E = 8
BX = 16
BY = 4
LANES = 128
ORDER = (3, 0, 1, 2)
MESH = pl.DeviceIdType.MESH


def minmod(a, b):
    return jnp.maximum(jnp.minimum(a, jnp.maximum(b, 0.0)), jnp.minimum(b, 0.0))


def split(x):
    high = x.astype(jnp.bfloat16)
    low = (x - high.astype(jnp.float32)).astype(jnp.bfloat16)
    return high, low


def pick(onehot2, x):
    high, low = split(x)
    return jnp.dot(onehot2, jnp.concatenate([high, low], axis=0), preferred_element_type=jnp.float32)


def iota(shape, dim):
    return lax.broadcasted_iota(jnp.int32, shape, dim)


def column(row):
    size = row.shape[1]
    diag = iota((size, size), 0) == iota((size, size), 1)
    return jnp.sum(jnp.where(diag, jnp.broadcast_to(row, (size, size)), 0.0), axis=1, keepdims=True)


def twice(onehot):
    half = jnp.where(onehot, 1.0, 0.0).astype(jnp.bfloat16)
    return jnp.concatenate([half, half], axis=1)


def refine_matrix(h):
    rows, cols = 2 * 64, 512
    i, j = iota((rows, cols), 0), iota((rows, cols), 1)
    parent = ((j >> 7) << 4) + (((j >> 4) & 3) << 2) + ((j >> 1) & 3) + h * 64
    match = jnp.where(i == parent, 1.0, 0.0)
    out = [match]
    for bit in (6, 3, 0):
        sign = jnp.where(((j >> bit) & 1) == 1, 0.25, -0.25)
        out.append(match * sign)
    return jnp.concatenate([m.astype(jnp.bfloat16) for m in out], axis=0)


def parent_slopes(c):
    lane = iota(c.shape, 1)
    out = [c]
    for bit in (4, 2, 0):
        step = 1 << bit
        inside = ((lane >> bit) & 3) != 0
        below = jnp.where(inside, c - pltpu.roll(c, step, 1), 0.0)
        above = pltpu.roll(below, LANES - step, 1)
        out.append(minmod(below, above))
    return out


def swap_lanes(rows):
    lane = iota(rows[0].shape, 1)
    rows = list(rows)
    for b in range(4):
        step = 8 << b
        upper = ((lane >> (3 + b)) & 1) == 1
        for i in range(16):
            if i & (1 << b):
                continue
            j = i | (1 << b)
            x, y = rows[i], rows[j]
            rows[i] = jnp.where(upper, pltpu.roll(y, step, 1), x)
            rows[j] = jnp.where(upper, y, pltpu.roll(x, LANES - step, 1))
    return rows


def step_x(u, c):
    lane = iota(u.shape, 1)
    first, last = lane == 0, lane == LANES - 1
    d = u - jnp.where(first, 0.0, pltpu.roll(u, 1, 1))
    above = jnp.where(last, -u, pltpu.roll(d, LANES - 1, 1))
    g = u + 0.5 * minmod(d, above)
    return c * (g - jnp.where(first, 0.0, pltpu.roll(g, 1, 1)))


def step_y(u, c):
    n = u.shape[0]
    row = iota(u.shape, 0)
    d = u - pltpu.roll(u, 1, 0)
    g = u + 0.5 * minmod(d, pltpu.roll(d, n - 1, 0))
    return jnp.where((row >= 2) & (row <= n - 2), c * (g - pltpu.roll(g, 1, 0)), 0.0)


def kernel(
    slabs, tiles, old_hbm, coarse_hbm, owner_hbm, refine_hbm, parent_hbm, courant_hbm,
    out, owner_ref, refine_ref, parent_ref, courant, old, coarse, csend, crecv, send, recv, matrix, stacked, interp, tmp, region,
    zlow, zhigh, ysend_up, ysend_down, ylow, yhigh,
    load_sem, csem, asend, arecv, zsem, ysend_sem, yrecv_sem,
):
    slab, tile = lax.axis_index("slab"), lax.axis_index("tile")
    fields, blocks, cells = old.shape
    groups = cells // LANES
    rows = BY * E
    share = blocks // tiles
    up, down = lax.rem(slab + 1, slabs), lax.rem(slab + slabs - 1, slabs)
    has_down, has_up = slab > 0, slab < slabs - 1
    has_left, has_right = tile > 0, tile < tiles - 1

    barrier = pltpu.get_barrier_semaphore()
    pl.semaphore_signal(barrier, inc=1, device_id={"slab": down}, device_id_type=MESH)

    @pl.when(has_up)
    def _():
        pl.semaphore_signal(barrier, inc=1, device_id={"slab": up}, device_id_type=MESH)

    for o in range(1, tiles):
        pl.semaphore_signal(
            barrier, inc=1, device_id={"tile": lax.rem(tile + o, tiles)}, device_id_type=MESH
        )
    sources = (owner_hbm, coarse_hbm, refine_hbm, parent_hbm, courant_hbm)
    targets = (owner_ref, coarse, refine_ref, parent_ref, courant)
    loads = [pltpu.make_async_copy(a, b, load_sem.at[i]) for i, (a, b) in enumerate(zip(sources, targets))]
    for load in loads:
        load.start()

    def load_old(g):
        at = pl.ds(g * LANES, LANES)
        return pltpu.make_async_copy(old_hbm.at[:, :, at], old.at[:, :, at], load_sem.at[5 + g])

    for g in ORDER:
        load_old(g).start()

    loads[0].wait()
    offset = owner_ref[0] - tile
    offset = jnp.where(offset < 0, offset + tiles, offset).astype(jnp.float32)
    square = (blocks, blocks)
    same = column(offset) == jnp.broadcast_to(offset, square)
    earlier = iota(square, 0) < iota(square, 1)
    rank = jnp.sum(jnp.where(same & earlier, 1.0, 0.0), axis=0, keepdims=True)
    place = offset * share + rank
    pack = twice(iota(square, 0).astype(jnp.float32) == jnp.broadcast_to(place, square))
    loads[1].wait()
    for f in range(fields):
        first = f // 2 * blocks
        if f % 2 or f + 1 < fields:
            csend[first:first + blocks, f % 2 * 64:f % 2 * 64 + 64] = coarse[f]
        else:
            csend[first:first + blocks // 2, :64] = coarse[f, :blocks // 2]
            csend[first:first + blocks // 2, 64:] = coarse[f, blocks // 2:]

    pl.semaphore_wait(barrier, tiles + jnp.minimum(slab, 1))

    send_coarse = pltpu.make_async_remote_copy(
        csend, crecv, csem.at[0], csem.at[1], device_id={"slab": up}, device_id_type=MESH
    )
    send_coarse.start()

    def exchange(g, o):
        return pltpu.make_async_remote_copy(
            send.at[g, :, o], recv.at[g, :, o], asend.at[g, o], arecv.at[g, o],
            device_id={"tile": lax.rem(tile + o, tiles)}, device_id_type=MESH,
        )

    def send_group(g):
        for o in sorted(range(1, tiles), key=lambda o: -min(o, tiles - o)):
            exchange(g, o).start()

    def sent_group(g):
        for o in range(1, tiles):
            exchange(g, o).wait_send()

    for n, g in enumerate(ORDER):
        load_old(g).wait()
        for f in range(fields):
            packed = pick(pack, old[f, :, g * LANES:(g + 1) * LANES])
            send[g, f] = packed.reshape(tiles, share, LANES)
            recv[g, f, 0] = packed[:share]
        if n == 0:
            send_group(g)

    @pl.when(jnp.logical_not(has_down))
    def _():
        zlow[...] = jnp.zeros_like(zlow)

    @pl.when(jnp.logical_not(has_up))
    def _():
        zhigh[...] = jnp.zeros_like(zhigh)

    @pl.when(jnp.logical_not(has_left))
    def _():
        ylow[...] = jnp.zeros_like(ylow)

    @pl.when(jnp.logical_not(has_right))
    def _():
        yhigh[...] = jnp.zeros_like(yhigh)

    for load in loads[2:]:
        load.wait()
    unpack_at = column(place) == iota(square, 1).astype(jnp.float32)
    refine = column(refine_ref[0].astype(jnp.float32)) > 0.5
    unpack = twice(unpack_at & ~refine)
    parents = twice((column(parent_ref[0].astype(jnp.float32)) == iota(square, 1).astype(jnp.float32)) & refine)
    for h in range(2):
        matrix[h] = refine_matrix(h)
    sent_group(ORDER[0])
    send_group(ORDER[1])
    send_group(ORDER[2])
    send_coarse.wait_recv()
    for p in range((fields + 1) // 2):
        first = p * blocks
        if 2 * p + 1 < fields:
            pair = crecv[first:first + blocks]
        else:
            pair = crecv[first:first + blocks // 2]
            pair = jnp.concatenate([pair, pltpu.roll(pair, 64, 1)], axis=0)
        parts = [split(part) for part in parent_slopes(pick(parents, pair))]
        for n in range(2):
            part = jnp.concatenate([part[n] for part in parts], axis=1)
            at = (2 * p + n) * blocks
            stacked[at:at + blocks] = part

    def refined(g):
        columns = slice(g * LANES, (g + 1) * LANES)
        for h in range(2):
            count = (fields + 1 - h) // 2
            both = jnp.dot(
                stacked[:2 * count * blocks], matrix[h, :, columns], preferred_element_type=jnp.float32
            )
            for p in range(count):
                at = 2 * p * blocks
                interp[g, 2 * p + h] = both[at:at + blocks] + both[at + blocks:at + 2 * blocks]

    send_up = pltpu.make_async_remote_copy(
        region.at[E - 2:E], zlow, zsem.at[0], zsem.at[1], device_id={"slab": up}, device_id_type=MESH
    )
    send_down = pltpu.make_async_remote_copy(
        region.at[0:1], zhigh, zsem.at[2], zsem.at[3], device_id={"slab": down}, device_id_type=MESH
    )

    def send_right(g):
        return pltpu.make_async_remote_copy(
            ysend_up.at[2 * g:2 * g + 2], ylow.at[2 * g:2 * g + 2], ysend_sem.at[0, g], yrecv_sem.at[0, g],
            device_id={"tile": lax.rem(tile + 1, tiles)}, device_id_type=MESH,
        )

    def send_left(g):
        return pltpu.make_async_remote_copy(
            ysend_down.at[2 * g:2 * g + 2], yhigh.at[2 * g:2 * g + 2], ysend_sem.at[1, g], yrecv_sem.at[1, g],
            device_id={"tile": lax.rem(tile + tiles - 1, tiles)}, device_id_type=MESH,
        )

    def at(f, z):
        return pl.ds(pl.multiple_of((f * E + z) * rows, rows), rows)

    def field_rows(f):
        return pl.ds(pl.multiple_of(f * rows, rows), rows)

    for g in ORDER:
        refined(g)
        for o in range(1, tiles):
            exchange(g, o).wait_recv()
        for f in range(fields):
            moved = pick(unpack, recv[g, f].reshape(blocks, LANES))
            tmp[g, f * blocks:(f + 1) * blocks] = moved + interp[g, f]
        turned = swap_lanes([tmp[g, pl.ds(b, fields * BY, stride=BX), :] for b in range(BX)])
        for j in range(BX):
            region[2 * g + j // E, pl.ds(j % E, fields * BY, stride=E), :] = turned[j]
        if g == 3:
            pl.when(has_up)(send_up.start)
            send_group(ORDER[3])
        if g == 0:
            pl.when(has_down)(send_down.start)
        for z in (2 * g, 2 * g + 1):
            for i in range(2):
                ysend_up[z, i] = region[z, pl.ds(rows - 2 + i, fields, stride=rows), :]
            ysend_down[z, 0] = region[z, pl.ds(0, fields, stride=rows), :]
        pl.when(has_right)(send_right(g).start)
        pl.when(has_left)(send_left(g).start)

        def along_xy(f, carry, g=g):
            for z in (2 * g, 2 * g + 1):
                u = region[z, field_rows(f), :]
                out[at(f, z), :] = u - step_x(u, courant[2, f]) - step_y(u, courant[1, f])
            return carry

        lax.fori_loop(0, fields, along_xy, 0, unroll=True)

    def along_z(f, carry):
        c = courant[0, f]
        u = [region[z, field_rows(f), :] for z in range(E)]
        d = [None] + [u[z] - u[z - 1] for z in range(1, E)]
        g = [None] + [u[z] + 0.5 * minmod(d[z], d[z + 1]) for z in range(1, E - 1)]
        for z in range(2, E - 1):
            out[at(f, z), :] -= c * (g[z] - g[z - 1])
        return carry

    lax.fori_loop(0, fields, along_z, 0, unroll=True)

    for g in ORDER:
        pl.when(has_left)(send_right(g).wait_recv)
        pl.when(has_right)(send_left(g).wait_recv)

    number = iota((fields, LANES), 0)
    c = jnp.zeros((fields, LANES), jnp.float32)
    for f in range(fields):
        c = jnp.where(number == f, courant[1, f], c)

    def face(u, below, above):
        return u + 0.5 * minmod(below, above)

    for z in range(E):
        u = {y: region[z, pl.ds(y % rows, fields, stride=rows), :] for y in (0, 1, 2, -3, -2, -1)}
        low2, low1, high = ylow[z, 0], ylow[z, 1], yhigh[z, 0]
        d0, d1 = u[0] - low1, u[1] - u[0]
        g = {
            -1: face(low1, low1 - low2, d0),
            0: face(u[0], d0, d1),
            1: face(u[1], d1, u[2] - u[1]),
        }
        d = u[-1] - u[-2]
        g[rows - 2], g[rows - 1] = face(u[-2], u[-2] - u[-3], d), face(u[-1], d, high - u[-1])
        for y in (0, 1, rows - 1):
            out[pl.ds(z * rows + y, fields, stride=E * rows), :] -= c * (g[y] - g[y - 1])

    pl.when(has_down)(send_up.wait_recv)
    pl.when(has_up)(send_down.wait_recv)

    def edges(f, carry):
        c = courant[0, f]
        here = field_rows(f)
        u = {z: region[z, here, :] for z in (0, 1, 2, E - 3, E - 2, E - 1)}
        u[-2], u[-1], u[E] = zlow[0, here, :], zlow[1, here, :], zhigh[0, here, :]
        d = {z: u[z] - u[z - 1] for z in (-1, 0, 1, 2, E - 2, E - 1, E)}
        g = {z: u[z] + 0.5 * minmod(d[z], d[z + 1]) for z in (-1, 0, 1, E - 2, E - 1)}
        for z in (0, 1, E - 1):
            out[at(f, z), :] -= c * (g[z] - g[z - 1])
        return carry

    lax.fori_loop(0, fields, edges, 0, unroll=True)

    send_coarse.wait_send()
    for g in ORDER[1:]:
        sent_group(g)
    for g in ORDER:
        pl.when(has_right)(send_right(g).wait_send)
        pl.when(has_left)(send_left(g).wait_send)
    pl.when(has_up)(send_up.wait_send)
    pl.when(has_down)(send_down.wait_send)


def local(slabs, tiles, old_fine, coarse_fine, old_owner, new_refine, parent_map, courant):
    blocks, fields, cells = old_fine.shape
    half = coarse_fine.shape[2]
    groups = cells // LANES
    share = blocks // tiles
    rows = BY * E
    f32 = jnp.float32
    vmem = pl.BlockSpec(memory_space=pltpu.VMEM)
    hbm = pl.BlockSpec(memory_space=pltpu.HBM)
    dma = pltpu.SemaphoreType.DMA
    operands = (
        jnp.transpose(old_fine, (1, 0, 2)),
        jnp.transpose(coarse_fine, (1, 0, 2)),
        old_owner,
        new_refine,
        parent_map,
        courant,
    )
    stepped = pl.pallas_call(
        functools.partial(kernel, slabs, tiles),
        out_shape=pltpu.VMEM((fields * E * rows, BX * E), f32),
        in_specs=[hbm] * 6,
        out_specs=vmem,
        scratch_shapes=[
            pltpu.VMEM(old_owner.shape, jnp.int32),
            pltpu.VMEM(new_refine.shape, jnp.int32),
            pltpu.VMEM(parent_map.shape, jnp.int32),
            pltpu.SMEM(courant.shape, f32),
            pltpu.VMEM((fields, blocks, cells), f32),
            pltpu.VMEM((fields, blocks, half), f32),
            pltpu.VMEM((fields * blocks // 2, LANES), f32),
            pltpu.VMEM((fields * blocks // 2, LANES), f32),
            pltpu.VMEM((groups, fields, tiles, share, LANES), f32),
            pltpu.VMEM((groups, fields, tiles, share, LANES), f32),
            pltpu.VMEM((2, 4 * LANES, cells), jnp.bfloat16),
            pltpu.VMEM(((fields + 1) // 2 * 2 * blocks, 4 * LANES), jnp.bfloat16),
            pltpu.VMEM((groups, fields, blocks, LANES), f32),
            pltpu.VMEM((groups, fields * blocks, LANES), f32),
            pltpu.VMEM((E, fields * rows, LANES), f32),
            pltpu.VMEM((2, fields * rows, LANES), f32),
            pltpu.VMEM((1, fields * rows, LANES), f32),
            pltpu.VMEM((E, 2, fields, LANES), f32),
            pltpu.VMEM((E, 1, fields, LANES), f32),
            pltpu.VMEM((E, 2, fields, LANES), f32),
            pltpu.VMEM((E, 1, fields, LANES), f32),
            dma((5 + groups,)),
            dma((2,)),
            dma((groups, tiles)),
            dma((groups, tiles)),
            dma((4,)),
            dma((2, groups)),
            dma((2, groups)),
        ],
        compiler_params=pltpu.CompilerParams(
            collective_id=0, has_side_effects=True, vmem_limit_bytes=32 * 1024 * 1024
        ),
        cost_estimate=pl.CostEstimate(flops=20_000_000, bytes_accessed=2_000_000, transcendentals=0),
    )(*(pltpu.with_memory_space_constraint(operand, pltpu.HBM) for operand in operands))
    return stepped.reshape(fields, E, rows, BX * E)


def solution(mesh):
    in_specs = (
        P(("slab", "tile"), None, None),
        P(("slab", "tile"), None, None),
        P("slab", "tile", None),
        P("slab", "tile", None),
        P("slab", "tile", None),
        P(),
    )
    out_specs = P(None, "slab", "tile", None)
    body = functools.partial(local, mesh.shape["slab"], mesh.shape["tile"])
    return jax.shard_map(body, mesh=mesh, in_specs=in_specs, out_specs=out_specs, check_vma=False)
```

```python
import functools

import jax
import jax.numpy as jnp
from jax import lax
from jax.experimental import pallas as pl
from jax.experimental.pallas import tpu as pltpu
from jax.sharding import PartitionSpec as P

E = 8
BX = 16
BY = 4
LANES = 128
ORDER = (3, 0, 1, 2)
MESH = pl.DeviceIdType.MESH


def minmod(a, b):
    return jnp.maximum(jnp.minimum(a, jnp.maximum(b, 0.0)), jnp.minimum(b, 0.0))


def split(x):
    high = x.astype(jnp.bfloat16)
    low = (x - high.astype(jnp.float32)).astype(jnp.bfloat16)
    return high, low


def pick(onehot2, x):
    high, low = split(x)
    return jnp.dot(onehot2, jnp.concatenate([high, low], axis=0), preferred_element_type=jnp.float32)


def iota(shape, dim):
    return lax.broadcasted_iota(jnp.int32, shape, dim)


def column(row):
    size = row.shape[1]
    diag = iota((size, size), 0) == iota((size, size), 1)
    return jnp.sum(jnp.where(diag, jnp.broadcast_to(row, (size, size)), 0.0), axis=1, keepdims=True)


def twice(onehot):
    half = jnp.where(onehot, 1.0, 0.0).astype(jnp.bfloat16)
    return jnp.concatenate([half, half], axis=1)


def refine_matrix(h):
    rows, cols = 2 * 64, 512
    i, j = iota((rows, cols), 0), iota((rows, cols), 1)
    parent = ((j >> 7) << 4) + (((j >> 4) & 3) << 2) + ((j >> 1) & 3) + h * 64
    match = jnp.where(i == parent, 1.0, 0.0)
    out = [match]
    for bit in (6, 3, 0):
        sign = jnp.where(((j >> bit) & 1) == 1, 0.25, -0.25)
        out.append(match * sign)
    return jnp.concatenate([m.astype(jnp.bfloat16) for m in out], axis=0)


def parent_slopes(c):
    lane = iota(c.shape, 1)
    out = [c]
    for bit in (4, 2, 0):
        step = 1 << bit
        inside = ((lane >> bit) & 3) != 0
        below = jnp.where(inside, c - pltpu.roll(c, step, 1), 0.0)
        above = pltpu.roll(below, LANES - step, 1)
        out.append(minmod(below, above))
    return out


def swap_lanes(rows):
    lane = iota(rows[0].shape, 1)
    rows = list(rows)
    for b in range(4):
        step = 8 << b
        upper = ((lane >> (3 + b)) & 1) == 1
        for i in range(16):
            if i & (1 << b):
                continue
            j = i | (1 << b)
            x, y = rows[i], rows[j]
            rows[i] = jnp.where(upper, pltpu.roll(y, step, 1), x)
            rows[j] = jnp.where(upper, y, pltpu.roll(x, LANES - step, 1))
    return rows


def step_x(u, c):
    lane = iota(u.shape, 1)
    first, last = lane == 0, lane == LANES - 1
    d = u - jnp.where(first, 0.0, pltpu.roll(u, 1, 1))
    above = jnp.where(last, -u, pltpu.roll(d, LANES - 1, 1))
    g = u + 0.5 * minmod(d, above)
    return c * (g - jnp.where(first, 0.0, pltpu.roll(g, 1, 1)))


def step_y(u, c):
    n = u.shape[0]
    row = iota(u.shape, 0)
    d = u - pltpu.roll(u, 1, 0)
    g = u + 0.5 * minmod(d, pltpu.roll(d, n - 1, 0))
    return jnp.where((row >= 2) & (row <= n - 2), c * (g - pltpu.roll(g, 1, 0)), 0.0)


def kernel(
    slabs, tiles, old_hbm, coarse_hbm, owner_hbm, refine_hbm, parent_hbm, courant_hbm,
    out, owner_ref, refine_ref, parent_ref, courant, old, coarse, csend, crecv, send, recv, matrix, stacked, interp, tmp, region,
    zlow, zhigh, ysend_up, ysend_down, ylow, yhigh,
    load_sem, csem, asend, arecv, zsem, ysend_sem, yrecv_sem,
):
    slab, tile = lax.axis_index("slab"), lax.axis_index("tile")
    fields, blocks, cells = old.shape
    groups = cells // LANES
    rows = BY * E
    share = blocks // tiles
    up, down = lax.rem(slab + 1, slabs), lax.rem(slab + slabs - 1, slabs)
    has_down, has_up = slab > 0, slab < slabs - 1
    has_left, has_right = tile > 0, tile < tiles - 1

    barrier = pltpu.get_barrier_semaphore()
    pl.semaphore_signal(barrier, inc=1, device_id={"slab": down}, device_id_type=MESH)

    @pl.when(has_up)
    def _():
        pl.semaphore_signal(barrier, inc=1, device_id={"slab": up}, device_id_type=MESH)

    for o in range(1, tiles):
        pl.semaphore_signal(
            barrier, inc=1, device_id={"tile": lax.rem(tile + o, tiles)}, device_id_type=MESH
        )
    sources = (owner_hbm, coarse_hbm, refine_hbm, parent_hbm, courant_hbm)
    targets = (owner_ref, coarse, refine_ref, parent_ref, courant)
    loads = [pltpu.make_async_copy(a, b, load_sem.at[i]) for i, (a, b) in enumerate(zip(sources, targets))]
    for load in loads:
        load.start()

    def load_old(g):
        at = pl.ds(g * LANES, LANES)
        return pltpu.make_async_copy(old_hbm.at[:, :, at], old.at[:, :, at], load_sem.at[5 + g])

    for g in ORDER:
        load_old(g).start()

    loads[0].wait()
    offset = owner_ref[0] - tile
    offset = jnp.where(offset < 0, offset + tiles, offset).astype(jnp.float32)
    square = (blocks, blocks)
    same = column(offset) == jnp.broadcast_to(offset, square)
    earlier = iota(square, 0) < iota(square, 1)
    rank = jnp.sum(jnp.where(same & earlier, 1.0, 0.0), axis=0, keepdims=True)
    place = offset * share + rank
    pack = twice(iota(square, 0).astype(jnp.float32) == jnp.broadcast_to(place, square))
    loads[1].wait()
    for f in range(fields):
        first = f // 2 * blocks
        if f % 2 or f + 1 < fields:
            csend[first:first + blocks, f % 2 * 64:f % 2 * 64 + 64] = coarse[f]
        else:
            csend[first:first + blocks // 2, :64] = coarse[f, :blocks // 2]
            csend[first:first + blocks // 2, 64:] = coarse[f, blocks // 2:]

    pl.semaphore_wait(barrier, tiles + jnp.minimum(slab, 1))

    send_coarse = pltpu.make_async_remote_copy(
        csend, crecv, csem.at[0], csem.at[1], device_id={"slab": up}, device_id_type=MESH
    )
    send_coarse.start()

    def exchange(g, o):
        return pltpu.make_async_remote_copy(
            send.at[g, :, o], recv.at[g, :, o], asend.at[g, o], arecv.at[g, o],
            device_id={"tile": lax.rem(tile + o, tiles)}, device_id_type=MESH,
        )

    def send_group(g):
        for o in sorted(range(1, tiles), key=lambda o: -min(o, tiles - o)):
            exchange(g, o).start()

    def sent_group(g):
        for o in range(1, tiles):
            exchange(g, o).wait_send()

    for n, g in enumerate(ORDER):
        load_old(g).wait()
        for f in range(fields):
            packed = pick(pack, old[f, :, g * LANES:(g + 1) * LANES])
            send[g, f] = packed.reshape(tiles, share, LANES)
            recv[g, f, 0] = packed[:share]
        if n == 0:
            send_group(g)

    @pl.when(jnp.logical_not(has_down))
    def _():
        zlow[...] = jnp.zeros_like(zlow)

    @pl.when(jnp.logical_not(has_up))
    def _():
        zhigh[...] = jnp.zeros_like(zhigh)

    @pl.when(jnp.logical_not(has_left))
    def _():
        ylow[...] = jnp.zeros_like(ylow)

    @pl.when(jnp.logical_not(has_right))
    def _():
        yhigh[...] = jnp.zeros_like(yhigh)

    for load in loads[2:]:
        load.wait()
    unpack_at = column(place) == iota(square, 1).astype(jnp.float32)
    refine = column(refine_ref[0].astype(jnp.float32)) > 0.5
    unpack = twice(unpack_at & ~refine)
    parents = twice((column(parent_ref[0].astype(jnp.float32)) == iota(square, 1).astype(jnp.float32)) & refine)
    for h in range(2):
        matrix[h] = refine_matrix(h)
    sent_group(ORDER[0])
    send_group(ORDER[1])
    send_group(ORDER[2])
    pl.when(jnp.logical_not(has_down))(lambda: send_group(ORDER[3]))
    send_coarse.wait_recv()
    for p in range((fields + 1) // 2):
        first = p * blocks
        if 2 * p + 1 < fields:
            pair = crecv[first:first + blocks]
        else:
            pair = crecv[first:first + blocks // 2]
            pair = jnp.concatenate([pair, pltpu.roll(pair, 64, 1)], axis=0)
        parts = [split(part) for part in parent_slopes(pick(parents, pair))]
        for n in range(2):
            part = jnp.concatenate([part[n] for part in parts], axis=1)
            at = (2 * p + n) * blocks
            stacked[at:at + blocks] = part

    def refined(g):
        columns = slice(g * LANES, (g + 1) * LANES)
        for h in range(2):
            count = (fields + 1 - h) // 2
            both = jnp.dot(
                stacked[:2 * count * blocks], matrix[h, :, columns], preferred_element_type=jnp.float32
            )
            for p in range(count):
                at = 2 * p * blocks
                interp[g, 2 * p + h] = both[at:at + blocks] + both[at + blocks:at + 2 * blocks]

    send_up = pltpu.make_async_remote_copy(
        region.at[E - 2:E], zlow, zsem.at[0], zsem.at[1], device_id={"slab": up}, device_id_type=MESH
    )
    send_down = pltpu.make_async_remote_copy(
        region.at[0:1], zhigh, zsem.at[2], zsem.at[3], device_id={"slab": down}, device_id_type=MESH
    )

    def send_right(g):
        return pltpu.make_async_remote_copy(
            ysend_up.at[2 * g:2 * g + 2], ylow.at[2 * g:2 * g + 2], ysend_sem.at[0, g], yrecv_sem.at[0, g],
            device_id={"tile": lax.rem(tile + 1, tiles)}, device_id_type=MESH,
        )

    def send_left(g):
        return pltpu.make_async_remote_copy(
            ysend_down.at[2 * g:2 * g + 2], yhigh.at[2 * g:2 * g + 2], ysend_sem.at[1, g], yrecv_sem.at[1, g],
            device_id={"tile": lax.rem(tile + tiles - 1, tiles)}, device_id_type=MESH,
        )

    def at(f, z):
        return pl.ds(pl.multiple_of((f * E + z) * rows, rows), rows)

    def field_rows(f):
        return pl.ds(pl.multiple_of(f * rows, rows), rows)

    for g in ORDER:
        refined(g)
        for o in range(1, tiles):
            exchange(g, o).wait_recv()
        for f in range(fields):
            moved = pick(unpack, recv[g, f].reshape(blocks, LANES))
            tmp[g, f * blocks:(f + 1) * blocks] = moved + interp[g, f]
        turned = swap_lanes([tmp[g, pl.ds(b, fields * BY, stride=BX), :] for b in range(BX)])
        for j in range(BX):
            region[2 * g + j // E, pl.ds(j % E, fields * BY, stride=E), :] = turned[j]
        if g == 3:
            pl.when(has_up)(send_up.start)
            pl.when(has_down)(lambda: send_group(ORDER[3]))
        if g == 0:
            pl.when(has_down)(send_down.start)
        for z in (2 * g, 2 * g + 1):
            for i in range(2):
                ysend_up[z, i] = region[z, pl.ds(rows - 2 + i, fields, stride=rows), :]
            ysend_down[z, 0] = region[z, pl.ds(0, fields, stride=rows), :]
        pl.when(has_right)(send_right(g).start)
        pl.when(has_left)(send_left(g).start)

        def along_xy(f, carry, g=g):
            for z in (2 * g, 2 * g + 1):
                u = region[z, field_rows(f), :]
                out[at(f, z), :] = u - step_x(u, courant[2, f]) - step_y(u, courant[1, f])
            return carry

        lax.fori_loop(0, fields, along_xy, 0, unroll=True)

    def along_z(f, carry):
        c = courant[0, f]
        u = [region[z, field_rows(f), :] for z in range(E)]
        d = [None] + [u[z] - u[z - 1] for z in range(1, E)]
        g = [None] + [u[z] + 0.5 * minmod(d[z], d[z + 1]) for z in range(1, E - 1)]
        for z in range(2, E - 1):
            out[at(f, z), :] -= c * (g[z] - g[z - 1])
        return carry

    lax.fori_loop(0, fields, along_z, 0, unroll=True)

    for g in ORDER:
        pl.when(has_left)(send_right(g).wait_recv)
        pl.when(has_right)(send_left(g).wait_recv)

    number = iota((fields, LANES), 0)
    c = jnp.zeros((fields, LANES), jnp.float32)
    for f in range(fields):
        c = jnp.where(number == f, courant[1, f], c)

    def face(u, below, above):
        return u + 0.5 * minmod(below, above)

    for z in range(E):
        u = {y: region[z, pl.ds(y % rows, fields, stride=rows), :] for y in (0, 1, 2, -3, -2, -1)}
        low2, low1, high = ylow[z, 0], ylow[z, 1], yhigh[z, 0]
        d0, d1 = u[0] - low1, u[1] - u[0]
        g = {
            -1: face(low1, low1 - low2, d0),
            0: face(u[0], d0, d1),
            1: face(u[1], d1, u[2] - u[1]),
        }
        d = u[-1] - u[-2]
        g[rows - 2], g[rows - 1] = face(u[-2], u[-2] - u[-3], d), face(u[-1], d, high - u[-1])
        for y in (0, 1, rows - 1):
            out[pl.ds(z * rows + y, fields, stride=E * rows), :] -= c * (g[y] - g[y - 1])

    pl.when(has_down)(send_up.wait_recv)
    pl.when(has_up)(send_down.wait_recv)

    def edges(f, carry):
        c = courant[0, f]
        here = field_rows(f)
        u = {z: region[z, here, :] for z in (0, 1, 2, E - 3, E - 2, E - 1)}
        u[-2], u[-1], u[E] = zlow[0, here, :], zlow[1, here, :], zhigh[0, here, :]
        d = {z: u[z] - u[z - 1] for z in (-1, 0, 1, 2, E - 2, E - 1, E)}
        g = {z: u[z] + 0.5 * minmod(d[z], d[z + 1]) for z in (-1, 0, 1, E - 2, E - 1)}
        for z in (0, 1, E - 1):
            out[at(f, z), :] -= c * (g[z] - g[z - 1])
        return carry

    lax.fori_loop(0, fields, edges, 0, unroll=True)

    send_coarse.wait_send()
    for g in ORDER[1:]:
        sent_group(g)
    for g in ORDER:
        pl.when(has_right)(send_right(g).wait_send)
        pl.when(has_left)(send_left(g).wait_send)
    pl.when(has_up)(send_up.wait_send)
    pl.when(has_down)(send_down.wait_send)


def local(slabs, tiles, old_fine, coarse_fine, old_owner, new_refine, parent_map, courant):
    blocks, fields, cells = old_fine.shape
    half = coarse_fine.shape[2]
    groups = cells // LANES
    share = blocks // tiles
    rows = BY * E
    f32 = jnp.float32
    vmem = pl.BlockSpec(memory_space=pltpu.VMEM)
    hbm = pl.BlockSpec(memory_space=pltpu.HBM)
    dma = pltpu.SemaphoreType.DMA
    operands = (
        jnp.transpose(old_fine, (1, 0, 2)),
        jnp.transpose(coarse_fine, (1, 0, 2)),
        old_owner,
        new_refine,
        parent_map,
        courant,
    )
    stepped = pl.pallas_call(
        functools.partial(kernel, slabs, tiles),
        out_shape=pltpu.VMEM((fields * E * rows, BX * E), f32),
        in_specs=[hbm] * 6,
        out_specs=vmem,
        scratch_shapes=[
            pltpu.VMEM(old_owner.shape, jnp.int32),
            pltpu.VMEM(new_refine.shape, jnp.int32),
            pltpu.VMEM(parent_map.shape, jnp.int32),
            pltpu.SMEM(courant.shape, f32),
            pltpu.VMEM((fields, blocks, cells), f32),
            pltpu.VMEM((fields, blocks, half), f32),
            pltpu.VMEM((fields * blocks // 2, LANES), f32),
            pltpu.VMEM((fields * blocks // 2, LANES), f32),
            pltpu.VMEM((groups, fields, tiles, share, LANES), f32),
            pltpu.VMEM((groups, fields, tiles, share, LANES), f32),
            pltpu.VMEM((2, 4 * LANES, cells), jnp.bfloat16),
            pltpu.VMEM(((fields + 1) // 2 * 2 * blocks, 4 * LANES), jnp.bfloat16),
            pltpu.VMEM((groups, fields, blocks, LANES), f32),
            pltpu.VMEM((groups, fields * blocks, LANES), f32),
            pltpu.VMEM((E, fields * rows, LANES), f32),
            pltpu.VMEM((2, fields * rows, LANES), f32),
            pltpu.VMEM((1, fields * rows, LANES), f32),
            pltpu.VMEM((E, 2, fields, LANES), f32),
            pltpu.VMEM((E, 1, fields, LANES), f32),
            pltpu.VMEM((E, 2, fields, LANES), f32),
            pltpu.VMEM((E, 1, fields, LANES), f32),
            dma((5 + groups,)),
            dma((2,)),
            dma((groups, tiles)),
            dma((groups, tiles)),
            dma((4,)),
            dma((2, groups)),
            dma((2, groups)),
        ],
        compiler_params=pltpu.CompilerParams(
            collective_id=0, has_side_effects=True, vmem_limit_bytes=32 * 1024 * 1024
        ),
        cost_estimate=pl.CostEstimate(flops=20_000_000, bytes_accessed=2_000_000, transcendentals=0),
    )(*(pltpu.with_memory_space_constraint(operand, pltpu.HBM) for operand in operands))
    return stepped.reshape(fields, E, rows, BX * E)


def solution(mesh):
    in_specs = (
        P(("slab", "tile"), None, None),
        P(("slab", "tile"), None, None),
        P("slab", "tile", None),
        P("slab", "tile", None),
        P("slab", "tile", None),
        P(),
    )
    out_specs = P(None, "slab", "tile", None)
    body = functools.partial(local, mesh.shape["slab"], mesh.shape["tile"])
    return jax.shard_map(body, mesh=mesh, in_specs=in_specs, out_specs=out_specs, check_vma=False)
```

```python
import functools

import jax
import jax.numpy as jnp
from jax import lax
from jax.experimental import pallas as pl
from jax.experimental.pallas import tpu as pltpu
from jax.sharding import PartitionSpec as P

E = 8
BX = 16
BY = 4
LANES = 128
ORDER = (3, 0, 1, 2)
MESH = pl.DeviceIdType.MESH


def minmod(a, b):
    return jnp.maximum(jnp.minimum(a, jnp.maximum(b, 0.0)), jnp.minimum(b, 0.0))


def split(x):
    high = x.astype(jnp.bfloat16)
    low = (x - high.astype(jnp.float32)).astype(jnp.bfloat16)
    return high, low


def pick(onehot2, x):
    high, low = split(x)
    return jnp.dot(onehot2, jnp.concatenate([high, low], axis=0), preferred_element_type=jnp.float32)


def iota(shape, dim):
    return lax.broadcasted_iota(jnp.int32, shape, dim)


def column(row):
    size = row.shape[1]
    diag = iota((size, size), 0) == iota((size, size), 1)
    return jnp.sum(jnp.where(diag, jnp.broadcast_to(row, (size, size)), 0.0), axis=1, keepdims=True)


def twice(onehot):
    half = jnp.where(onehot, 1.0, 0.0).astype(jnp.bfloat16)
    return jnp.concatenate([half, half], axis=1)


def refine_matrix(h):
    rows, cols = 2 * 64, 512
    i, j = iota((rows, cols), 0), iota((rows, cols), 1)
    parent = ((j >> 7) << 4) + (((j >> 4) & 3) << 2) + ((j >> 1) & 3) + h * 64
    match = jnp.where(i == parent, 1.0, 0.0)
    out = [match]
    for bit in (6, 3, 0):
        sign = jnp.where(((j >> bit) & 1) == 1, 0.25, -0.25)
        out.append(match * sign)
    return jnp.concatenate([m.astype(jnp.bfloat16) for m in out], axis=0)


def parent_slopes(c):
    lane = iota(c.shape, 1)
    out = [c]
    for bit in (4, 2, 0):
        step = 1 << bit
        inside = ((lane >> bit) & 3) != 0
        below = jnp.where(inside, c - pltpu.roll(c, step, 1), 0.0)
        above = pltpu.roll(below, LANES - step, 1)
        out.append(minmod(below, above))
    return out


def swap_lanes(rows):
    lane = iota(rows[0].shape, 1)
    rows = list(rows)
    for b in range(4):
        step = 8 << b
        upper = ((lane >> (3 + b)) & 1) == 1
        for i in range(16):
            if i & (1 << b):
                continue
            j = i | (1 << b)
            x, y = rows[i], rows[j]
            rows[i] = jnp.where(upper, pltpu.roll(y, step, 1), x)
            rows[j] = jnp.where(upper, y, pltpu.roll(x, LANES - step, 1))
    return rows


def step_x(u, c):
    lane = iota(u.shape, 1)
    first, last = lane == 0, lane == LANES - 1
    d = u - jnp.where(first, 0.0, pltpu.roll(u, 1, 1))
    above = jnp.where(last, -u, pltpu.roll(d, LANES - 1, 1))
    g = u + 0.5 * minmod(d, above)
    return c * (g - jnp.where(first, 0.0, pltpu.roll(g, 1, 1)))


def step_y(u, c):
    n = u.shape[0]
    row = iota(u.shape, 0)
    d = u - pltpu.roll(u, 1, 0)
    g = u + 0.5 * minmod(d, pltpu.roll(d, n - 1, 0))
    return jnp.where((row >= 2) & (row <= n - 2), c * (g - pltpu.roll(g, 1, 0)), 0.0)


def kernel(
    slabs, tiles, old_hbm, coarse_hbm, owner_hbm, refine_hbm, parent_hbm, courant_hbm,
    out, owner_ref, refine_ref, parent_ref, courant, old, coarse, csend, crecv, send, recv, matrix, stacked, interp, tmp, region,
    zlow, zhigh, ysend_up, ysend_down, ylow, yhigh,
    load_sem, csem, asend, arecv, zsem, ysend_sem, yrecv_sem,
):
    slab, tile = lax.axis_index("slab"), lax.axis_index("tile")
    fields, blocks, cells = old.shape
    groups = cells // LANES
    rows = BY * E
    share = blocks // tiles
    up, down = lax.rem(slab + 1, slabs), lax.rem(slab + slabs - 1, slabs)
    has_down, has_up = slab > 0, slab < slabs - 1
    has_left, has_right = tile > 0, tile < tiles - 1

    barrier = pltpu.get_barrier_semaphore()
    pl.semaphore_signal(barrier, inc=1, device_id={"slab": down}, device_id_type=MESH)

    @pl.when(has_up)
    def _():
        pl.semaphore_signal(barrier, inc=1, device_id={"slab": up}, device_id_type=MESH)

    for o in range(1, tiles):
        pl.semaphore_signal(
            barrier, inc=1, device_id={"tile": lax.rem(tile + o, tiles)}, device_id_type=MESH
        )
    sources = (owner_hbm, coarse_hbm, refine_hbm, parent_hbm, courant_hbm)
    targets = (owner_ref, coarse, refine_ref, parent_ref, courant)
    loads = [pltpu.make_async_copy(a, b, load_sem.at[i]) for i, (a, b) in enumerate(zip(sources, targets))]
    for load in loads:
        load.start()

    def load_old(g):
        at = pl.ds(g * LANES, LANES)
        return pltpu.make_async_copy(old_hbm.at[:, :, at], old.at[:, :, at], load_sem.at[5 + g])

    for g in ORDER:
        load_old(g).start()

    loads[0].wait()
    offset = owner_ref[0] - tile
    offset = jnp.where(offset < 0, offset + tiles, offset).astype(jnp.float32)
    square = (blocks, blocks)
    same = column(offset) == jnp.broadcast_to(offset, square)
    earlier = iota(square, 0) < iota(square, 1)
    rank = jnp.sum(jnp.where(same & earlier, 1.0, 0.0), axis=0, keepdims=True)
    place = offset * share + rank
    pack = twice(iota(square, 0).astype(jnp.float32) == jnp.broadcast_to(place, square))
    loads[1].wait()
    for f in range(fields):
        first = f // 2 * blocks
        if f % 2 or f + 1 < fields:
            csend[first:first + blocks, f % 2 * 64:f % 2 * 64 + 64] = coarse[f]
        else:
            csend[first:first + blocks // 2, :64] = coarse[f, :blocks // 2]
            csend[first:first + blocks // 2, 64:] = coarse[f, blocks // 2:]

    pl.semaphore_wait(barrier, tiles + jnp.minimum(slab, 1))

    send_coarse = pltpu.make_async_remote_copy(
        csend, crecv, csem.at[0], csem.at[1], device_id={"slab": up}, device_id_type=MESH
    )
    send_coarse.start()

    def exchange(g, o):
        return pltpu.make_async_remote_copy(
            send.at[g, :, o], recv.at[g, :, o], asend.at[g, o], arecv.at[g, o],
            device_id={"tile": lax.rem(tile + o, tiles)}, device_id_type=MESH,
        )

    def send_group(g):
        for o in sorted(range(1, tiles), key=lambda o: -min(o, tiles - o)):
            exchange(g, o).start()

    def sent_group(g):
        for o in range(1, tiles):
            exchange(g, o).wait_send()

    for n, g in enumerate(ORDER):
        load_old(g).wait()
        for f in range(fields):
            packed = pick(pack, old[f, :, g * LANES:(g + 1) * LANES])
            send[g, f] = packed.reshape(tiles, share, LANES)
            recv[g, f, 0] = packed[:share]
        if n == 0:
            send_group(g)

    @pl.when(jnp.logical_not(has_down))
    def _():
        zlow[...] = jnp.zeros_like(zlow)

    @pl.when(jnp.logical_not(has_up))
    def _():
        zhigh[...] = jnp.zeros_like(zhigh)

    @pl.when(jnp.logical_not(has_left))
    def _():
        ylow[...] = jnp.zeros_like(ylow)

    @pl.when(jnp.logical_not(has_right))
    def _():
        yhigh[...] = jnp.zeros_like(yhigh)

    for load in loads[2:]:
        load.wait()
    unpack_at = column(place) == iota(square, 1).astype(jnp.float32)
    refine = column(refine_ref[0].astype(jnp.float32)) > 0.5
    unpack = twice(unpack_at & ~refine)
    parents = twice((column(parent_ref[0].astype(jnp.float32)) == iota(square, 1).astype(jnp.float32)) & refine)
    for h in range(2):
        matrix[h] = refine_matrix(h)
    sent_group(ORDER[0])
    send_group(ORDER[1])
    send_group(ORDER[2])
    send_group(ORDER[3])
    send_coarse.wait_recv()
    for p in range((fields + 1) // 2):
        first = p * blocks
        if 2 * p + 1 < fields:
            pair = crecv[first:first + blocks]
        else:
            pair = crecv[first:first + blocks // 2]
            pair = jnp.concatenate([pair, pltpu.roll(pair, 64, 1)], axis=0)
        parts = [split(part) for part in parent_slopes(pick(parents, pair))]
        for n in range(2):
            part = jnp.concatenate([part[n] for part in parts], axis=1)
            at = (2 * p + n) * blocks
            stacked[at:at + blocks] = part

    def refined(g):
        columns = slice(g * LANES, (g + 1) * LANES)
        for h in range(2):
            count = (fields + 1 - h) // 2
            both = jnp.dot(
                stacked[:2 * count * blocks], matrix[h, :, columns], preferred_element_type=jnp.float32
            )
            for p in range(count):
                at = 2 * p * blocks
                interp[g, 2 * p + h] = both[at:at + blocks] + both[at + blocks:at + 2 * blocks]

    send_up = pltpu.make_async_remote_copy(
        region.at[E - 2:E], zlow, zsem.at[0], zsem.at[1], device_id={"slab": up}, device_id_type=MESH
    )
    send_down = pltpu.make_async_remote_copy(
        region.at[0:1], zhigh, zsem.at[2], zsem.at[3], device_id={"slab": down}, device_id_type=MESH
    )

    def send_right(g):
        return pltpu.make_async_remote_copy(
            ysend_up.at[2 * g:2 * g + 2], ylow.at[2 * g:2 * g + 2], ysend_sem.at[0, g], yrecv_sem.at[0, g],
            device_id={"tile": lax.rem(tile + 1, tiles)}, device_id_type=MESH,
        )

    def send_left(g):
        return pltpu.make_async_remote_copy(
            ysend_down.at[2 * g:2 * g + 2], yhigh.at[2 * g:2 * g + 2], ysend_sem.at[1, g], yrecv_sem.at[1, g],
            device_id={"tile": lax.rem(tile + tiles - 1, tiles)}, device_id_type=MESH,
        )

    def at(f, z):
        return pl.ds(pl.multiple_of((f * E + z) * rows, rows), rows)

    def field_rows(f):
        return pl.ds(pl.multiple_of(f * rows, rows), rows)

    for g in ORDER:
        refined(g)
        for o in range(1, tiles):
            exchange(g, o).wait_recv()
        for f in range(fields):
            moved = pick(unpack, recv[g, f].reshape(blocks, LANES))
            tmp[g, f * blocks:(f + 1) * blocks] = moved + interp[g, f]
        turned = swap_lanes([tmp[g, pl.ds(b, fields * BY, stride=BX), :] for b in range(BX)])
        for j in range(BX):
            region[2 * g + j // E, pl.ds(j % E, fields * BY, stride=E), :] = turned[j]
        if g == 3:
            pl.when(has_up)(send_up.start)
        if g == 0:
            pl.when(has_down)(send_down.start)
        for z in (2 * g, 2 * g + 1):
            for i in range(2):
                ysend_up[z, i] = region[z, pl.ds(rows - 2 + i, fields, stride=rows), :]
            ysend_down[z, 0] = region[z, pl.ds(0, fields, stride=rows), :]
        pl.when(has_right)(send_right(g).start)
        pl.when(has_left)(send_left(g).start)

        def along_xy(f, carry, g=g):
            for z in (2 * g, 2 * g + 1):
                u = region[z, field_rows(f), :]
                out[at(f, z), :] = u - step_x(u, courant[2, f]) - step_y(u, courant[1, f])
            return carry

        lax.fori_loop(0, fields, along_xy, 0, unroll=True)

    def along_z(f, carry):
        c = courant[0, f]
        u = [region[z, field_rows(f), :] for z in range(E)]
        d = [None] + [u[z] - u[z - 1] for z in range(1, E)]
        g = [None] + [u[z] + 0.5 * minmod(d[z], d[z + 1]) for z in range(1, E - 1)]
        for z in range(2, E - 1):
            out[at(f, z), :] -= c * (g[z] - g[z - 1])
        return carry

    lax.fori_loop(0, fields, along_z, 0, unroll=True)

    for g in ORDER:
        pl.when(has_left)(send_right(g).wait_recv)
        pl.when(has_right)(send_left(g).wait_recv)

    number = iota((fields, LANES), 0)
    c = jnp.zeros((fields, LANES), jnp.float32)
    for f in range(fields):
        c = jnp.where(number == f, courant[1, f], c)

    def face(u, below, above):
        return u + 0.5 * minmod(below, above)

    for z in range(E):
        u = {y: region[z, pl.ds(y % rows, fields, stride=rows), :] for y in (0, 1, 2, -3, -2, -1)}
        low2, low1, high = ylow[z, 0], ylow[z, 1], yhigh[z, 0]
        d0, d1 = u[0] - low1, u[1] - u[0]
        g = {
            -1: face(low1, low1 - low2, d0),
            0: face(u[0], d0, d1),
            1: face(u[1], d1, u[2] - u[1]),
        }
        d = u[-1] - u[-2]
        g[rows - 2], g[rows - 1] = face(u[-2], u[-2] - u[-3], d), face(u[-1], d, high - u[-1])
        for y in (0, 1, rows - 1):
            out[pl.ds(z * rows + y, fields, stride=E * rows), :] -= c * (g[y] - g[y - 1])

    pl.when(has_down)(send_up.wait_recv)
    pl.when(has_up)(send_down.wait_recv)

    def edges(f, carry):
        c = courant[0, f]
        here = field_rows(f)
        u = {z: region[z, here, :] for z in (0, 1, 2, E - 3, E - 2, E - 1)}
        u[-2], u[-1], u[E] = zlow[0, here, :], zlow[1, here, :], zhigh[0, here, :]
        d = {z: u[z] - u[z - 1] for z in (-1, 0, 1, 2, E - 2, E - 1, E)}
        g = {z: u[z] + 0.5 * minmod(d[z], d[z + 1]) for z in (-1, 0, 1, E - 2, E - 1)}
        for z in (0, 1, E - 1):
            out[at(f, z), :] -= c * (g[z] - g[z - 1])
        return carry

    lax.fori_loop(0, fields, edges, 0, unroll=True)

    send_coarse.wait_send()
    for g in ORDER[1:]:
        sent_group(g)
    for g in ORDER:
        pl.when(has_right)(send_right(g).wait_send)
        pl.when(has_left)(send_left(g).wait_send)
    pl.when(has_up)(send_up.wait_send)
    pl.when(has_down)(send_down.wait_send)


def local(slabs, tiles, old_fine, coarse_fine, old_owner, new_refine, parent_map, courant):
    blocks, fields, cells = old_fine.shape
    half = coarse_fine.shape[2]
    groups = cells // LANES
    share = blocks // tiles
    rows = BY * E
    f32 = jnp.float32
    vmem = pl.BlockSpec(memory_space=pltpu.VMEM)
    hbm = pl.BlockSpec(memory_space=pltpu.HBM)
    dma = pltpu.SemaphoreType.DMA
    operands = (
        jnp.transpose(old_fine, (1, 0, 2)),
        jnp.transpose(coarse_fine, (1, 0, 2)),
        old_owner,
        new_refine,
        parent_map,
        courant,
    )
    stepped = pl.pallas_call(
        functools.partial(kernel, slabs, tiles),
        out_shape=pltpu.VMEM((fields * E * rows, BX * E), f32),
        in_specs=[hbm] * 6,
        out_specs=vmem,
        scratch_shapes=[
            pltpu.VMEM(old_owner.shape, jnp.int32),
            pltpu.VMEM(new_refine.shape, jnp.int32),
            pltpu.VMEM(parent_map.shape, jnp.int32),
            pltpu.SMEM(courant.shape, f32),
            pltpu.VMEM((fields, blocks, cells), f32),
            pltpu.VMEM((fields, blocks, half), f32),
            pltpu.VMEM((fields * blocks // 2, LANES), f32),
            pltpu.VMEM((fields * blocks // 2, LANES), f32),
            pltpu.VMEM((groups, fields, tiles, share, LANES), f32),
            pltpu.VMEM((groups, fields, tiles, share, LANES), f32),
            pltpu.VMEM((2, 4 * LANES, cells), jnp.bfloat16),
            pltpu.VMEM(((fields + 1) // 2 * 2 * blocks, 4 * LANES), jnp.bfloat16),
            pltpu.VMEM((groups, fields, blocks, LANES), f32),
            pltpu.VMEM((groups, fields * blocks, LANES), f32),
            pltpu.VMEM((E, fields * rows, LANES), f32),
            pltpu.VMEM((2, fields * rows, LANES), f32),
            pltpu.VMEM((1, fields * rows, LANES), f32),
            pltpu.VMEM((E, 2, fields, LANES), f32),
            pltpu.VMEM((E, 1, fields, LANES), f32),
            pltpu.VMEM((E, 2, fields, LANES), f32),
            pltpu.VMEM((E, 1, fields, LANES), f32),
            dma((5 + groups,)),
            dma((2,)),
            dma((groups, tiles)),
            dma((groups, tiles)),
            dma((4,)),
            dma((2, groups)),
            dma((2, groups)),
        ],
        compiler_params=pltpu.CompilerParams(
            collective_id=0, has_side_effects=True, vmem_limit_bytes=32 * 1024 * 1024
        ),
        cost_estimate=pl.CostEstimate(flops=20_000_000, bytes_accessed=2_000_000, transcendentals=0),
    )(*(pltpu.with_memory_space_constraint(operand, pltpu.HBM) for operand in operands))
    return stepped.reshape(fields, E, rows, BX * E)


def solution(mesh):
    in_specs = (
        P(("slab", "tile"), None, None),
        P(("slab", "tile"), None, None),
        P("slab", "tile", None),
        P("slab", "tile", None),
        P("slab", "tile", None),
        P(),
    )
    out_specs = P(None, "slab", "tile", None)
    body = functools.partial(local, mesh.shape["slab"], mesh.shape["tile"])
    return jax.shard_map(body, mesh=mesh, in_specs=in_specs, out_specs=out_specs, check_vma=False)
```
